512 devices in a mesh: gx: 8 (over y, core), gy: 4 (over x), gz: 16 (over z).
Axes of the slice: x: 4, y: 4, z: 16, core: 2. Of those that a mesh axis runs over, the one named last changes fastest.
Arguments:
- volume: bfloat16 [256, 512, 4096], P('gz', 'gx', 'gy'), may hold values from 0 to 1
- knot_bins: int32 [8], replicated, may hold values from 0 to 255, as said below
- tf_colour: float32 [3, 8], replicated, may hold values from 0 to 1
- tf_density: float32 [8], replicated, may hold values from 0.1 to 10
Outputs:
- image: float32 [3, 512, 4096], P(None, ('gx', 'gz'), 'gy')
- coverage: float32 [512, 4096], P(('gx', 'gz'), 'gy')
The draws below stay inside these ranges and needn't reach their ends.
Inputs may be any that keep to these rules, and one draw needn't show every extreme that they name: `knot_bins`: strictly increasing; the first is 0 and the last is 255.
All inputs are finite; a program needn't handle non-finite values.
Results may differ from the reference program's by a relative error of at most 0.0003.
Values may be sent and summed in bfloat16 or wider, within the bound.
No kernel may reach another device: no remote copies, remote signals or barrier semaphores. Data moves between devices by JAX's collectives and lax.ppermute only.
A program may use at most 64 MiB of HBM per device.

```python
import math
import jax
import jax.numpy as jnp
from jax import lax

BINS = 256
KNOTS = 8
NX = 512
NY = 4096
NZ = 256


def draw_knot_bins(key, part):
    key = jax.random.fold_in(key, 11)
    inner = jax.random.permutation(key, BINS - 2)[:KNOTS - 2] + 1
    inner = jnp.sort(inner).astype(jnp.int32)
    return jnp.concatenate([jnp.zeros((1,), jnp.int32), inner, jnp.full((1,), BINS - 1, jnp.int32)])


def levels(own_key, shape, split, low, largest):
    loudness, own = 1.0, jax.random.fold_in(own_key, 6)
    for axis_at, blocks in split:
        heights = jnp.exp(jax.random.uniform(jax.random.fold_in(own, axis_at), (blocks,), jnp.float32, low / len(split), largest / len(split)))
        loudness = loudness * jnp.repeat(heights, shape[axis_at] // blocks).reshape([-1 if axis == axis_at else 1 for axis in range(len(shape))])
    return loudness


def setup_inputs(seed: int = 0) -> dict:
    keys = jax.random.split(jax.random.key(seed), 5)
    return {
        "volume": jnp.clip(1.0 * jax.random.uniform(keys[0], (NZ, NX, NY), jnp.float32) ** levels(keys[0], (NZ, NX, NY), ((0, 16), (1, 8), (2, 4)), -0.2, 0.2), 0.0, 1.0).astype(jnp.bfloat16),
        "knot_bins": draw_knot_bins(jax.random.fold_in(keys[4], 71), 0),
        "tf_colour": jnp.clip(jax.random.uniform(keys[2], (3, KNOTS), jnp.float32, 0.0, 1.0), 0.0, 1.0),
        "tf_density": jnp.clip(jnp.exp(jax.random.uniform(keys[3], (KNOTS,), jnp.float32, math.log(0.1), math.log(10.0))), 0.1, 10.0),
    }


LIGHT_X = 1.0 / 3.0
LIGHT_Y = 2.0 / 3.0
LIGHT_Z = 2.0 / 3.0
AMBIENT = 0.2

def classify(window, knot_bins, tf_colour, tf_density, depth_total):
    center = window[1:-1, 1:-1, 1:-1]
    grad_x = window[1:-1, 2:, 1:-1] - window[1:-1, :-2, 1:-1]
    grad_y = window[1:-1, 1:-1, 2:] - window[1:-1, 1:-1, :-2]
    grad_z = window[2:, 1:-1, 1:-1] - window[:-2, 1:-1, 1:-1]
    facing = jnp.abs(LIGHT_X * grad_x + LIGHT_Y * grad_y + LIGHT_Z * grad_z)
    shading = AMBIENT + (1.0 - AMBIENT) * facing / jnp.sqrt(grad_x * grad_x + grad_y * grad_y + grad_z * grad_z + 1.0)
    scalar = center * (BINS - 1.0)
    knots = knot_bins.astype(jnp.float32)
    spans = knots[1:] - knots[:-1]
    ramp_terms = jnp.clip(scalar[None] - knots[:-1, None, None, None], 0.0, spans[:, None, None, None])
    table = jnp.concatenate([tf_colour, tf_density[None]], 0)
    slopes = (table[:, 1:] - table[:, :-1]) / spans[None]
    mapped = table[:, :1, None, None] + jnp.einsum('kzxy,ck->czxy', ramp_terms, slopes, precision=lax.Precision.HIGHEST)
    opacity_step = 1.0 - jnp.exp(-mapped[3] / depth_total)
    emitted = mapped[:3] * shading[None]
    return (opacity_step, emitted)

def reference(volume, knot_bins, tf_colour, tf_density):
    padded = jnp.pad(volume, 1)
    depth_total = float(NZ)

    def advance(carry, plane):
        colour, transmit = carry
        window = lax.dynamic_slice_in_dim(padded, plane, 3, 0).astype(jnp.float32)
        opacity_step, emitted = classify(window, knot_bins, tf_colour, tf_density, depth_total)
        colour = colour + transmit[None] * opacity_step[0][None] * emitted[:, 0]
        transmit = transmit * (1.0 - opacity_step[0])
        return ((colour, transmit), None)
    start = (jnp.zeros((3, NX, NY), jnp.float32), jnp.ones((NX, NY), jnp.float32))
    (colour, transmit), _ = lax.scan(advance, start, jnp.arange(NZ, dtype=jnp.int32))
    return (colour, 1.0 - transmit)
```

```python
import functools
import math

import jax
import jax.numpy as jnp
import numpy as np
from jax import lax
from jax.experimental import pallas as pl
from jax.experimental.pallas import tpu as pltpu
from jax.sharding import PartitionSpec as P

BINS = 256
KNOTS = 8
SEGMENTS = KNOTS - 1
AMBIENT = 0.2
LANES = 128
SUB = 8
GROUPS = 8
PITCH = 9

COLOUR_SPAN = 26.0
COVER_SPAN = 9.0
CODES = 65534.0


def colour_scale(colour_ref, channel):
    largest = colour_ref[channel, 0]
    for k in range(1, KNOTS):
        largest = jnp.maximum(largest, colour_ref[channel, k])
    return jnp.maximum(largest, 1e-30)


def encode(value, span):
    position = (jnp.log2(jnp.maximum(value, 2.0 ** (-span - 1.0))) + span) * (CODES / span) + 1.5
    return jnp.clip(position, 0.0, 65535.0).astype(jnp.int32)


def opacity_terms(largest):
    half = 0.5 * largest
    nodes = [half + half * math.cos(math.pi * (2 * i + 1) / 8.0) for i in range(4)]
    values = [-math.expm1(-y) / y for y in nodes]
    return [float(c) for c in np.polynomial.polynomial.polyfit(nodes, values, 3)]


def full(x):
    return jnp.full((SUB, LANES), x, jnp.float32)


def lanes_of(t):
    return slice(t * LANES, (t + 1) * LANES)


def lane_index():
    return lax.broadcasted_iota(jnp.int32, (SUB, LANES), 1)


def edges_kernel(x_low, x_high, y_low, y_high, z_low, z_high, x_out, y_out, front, rear, rows_x):
    depth = x_low.shape[0]
    cols = x_low.shape[2]
    for z in range(depth):
        low = x_low[z].astype(jnp.float32)
        high = x_high[z].astype(jnp.float32)
        rows_x[0, z:z + 1, :] = low[:1]
        rows_x[1, z:z + 1, :] = high[15:]
    x_out[...] = rows_x[...].astype(x_out.dtype)
    lane = lane_index()
    for i in range(GROUPS // 2):
        sides = [jnp.zeros((SUB, LANES), jnp.float32)] * 2
        for z in range(depth):
            low = y_low[z, 16 * i:16 * i + 16, :].astype(jnp.float32)
            high = y_high[z, 16 * i:16 * i + 16, :].astype(jnp.float32)
            for part in range(2):
                at = slice(8 * part, 8 * part + 8)
                sides[part] = jnp.where(lane == z, low[at, :1], sides[part])
                sides[part] = jnp.where(lane == depth + z, high[at, LANES - 1:], sides[part])
        for part in range(2):
            y_out[pl.ds(2 * i + part, SUB, stride=GROUPS), :] = sides[part]
    front[...] = z_low[0]
    rear[...] = z_high[0]


def spread_kernel(vol_ref, cells, grads):
    depth, rows, cols = vol_ref.shape
    lane = lax.broadcasted_iota(jnp.int32, (16, LANES), 1)
    tiles = cols // LANES

    def step(z, carry):
        for c in range(rows // 16):
            plane = vol_ref[z, 16 * c:16 * c + 16, :].astype(jnp.float32)
            left = pltpu.roll(plane, 1, 1)
            right = pltpu.roll(plane, cols - 1, 1)
            for t in range(tiles):
                l, r = left[:, lanes_of(t)], right[:, lanes_of(t)]
                if t == 0:
                    l = jnp.where(lane == 0, 0.0, l)
                if t == tiles - 1:
                    r = jnp.where(lane == LANES - 1, 0.0, r)
                across = r - l
                own = plane[:, lanes_of(t)]
                for part in range(2):
                    i = 2 * c + part
                    at = slice(8 * part, 8 * part + 8)
                    cells[t, z, pl.ds(i, SUB, stride=PITCH), :] = own[at]
                    grads[t, z, pl.ds(i, SUB, stride=PITCH), :] = across[at]
        return carry

    lax.fori_loop(0, depth, step, 0)


def prepare(consts, knots_ref, colour_ref, density_ref, depth_total):
    top = BINS - 1.0
    spans = []
    for k in range(SEGMENTS):
        low = full(knots_ref[k].astype(jnp.float32))
        high = full(knots_ref[k + 1].astype(jnp.float32))
        spans.append((high - low) * (1.0 / top))
        if k:
            consts[k - 1] = low / top
    consts[6] = full(density_ref[0]) * (1.0 / depth_total)
    for k in range(SEGMENTS):
        step = full(density_ref[k + 1]) - full(density_ref[k])
        consts[7 + k] = step * (1.0 / depth_total) / spans[k]
    for c in range(3):
        scale = full(colour_scale(colour_ref, c))
        consts[14 + 8 * c] = full(colour_ref[c, 0]) / scale
        for k in range(SEGMENTS):
            step = full(colour_ref[c, k + 1]) - full(colour_ref[c, k])
            consts[15 + 8 * c + k] = step / scale / spans[k]


def composite(consts, cell, grad_x, grad_y, depth, depth_total):
    c0, c1, c2, c3 = opacity_terms(10.0 / depth_total)
    points = [consts[k] for k in range(6)]
    first = consts[6]
    slopes = [consts[7 + k] for k in range(SEGMENTS)]
    transmit = jnp.ones((SUB, LANES), jnp.float32)
    weight = None
    moments = None
    earlier, now = cell(-1), cell(0)
    for z in range(depth):
        later = cell(z + 1)
        gx, gy, gz = grad_x(z), grad_y(z), later - earlier
        across = gy + gz
        facing = jnp.abs(gx + (across + across))
        shading = AMBIENT + facing * (
            ((1.0 - AMBIENT) / 3.0) * lax.rsqrt(gx * gx + gy * gy + (gz * gz + 1.0))
        )
        capped = [jnp.minimum(now, p) for p in points] + [now]
        ramps = [capped[0]] + [capped[k + 1] - capped[k] for k in range(6)]
        y = first
        for k in range(SEGMENTS):
            y = y + ramps[k] * slopes[k]
        taken = transmit * (y * (c0 + y * (c1 + y * (c2 + y * c3))))
        transmit = transmit - taken
        shaded = taken * shading
        if z == 0:
            weight = shaded
            moments = [shaded * r for r in ramps]
        else:
            weight = weight + shaded
            moments = [m + shaded * r for m, r in zip(moments, ramps)]
        earlier, now = now, later
    codes = []
    for c in range(3):
        value = weight * consts[14 + 8 * c]
        for k in range(SEGMENTS):
            value = value + moments[k] * consts[15 + 8 * c + k]
        codes.append(encode(value, COLOUR_SPAN))
    codes.append(encode(1.0 - transmit, COVER_SPAN))
    return codes[0] | (codes[1] << 16), codes[2] | (codes[3] << 16)


def store_words(out_ref, words, t, r, tiles):
    base = (r // 4) * (tiles * SUB) + t * SUB + r % 4
    out_ref[pl.ds(base, SUB, stride=2 * tiles * SUB), :] = words[0]
    out_ref[pl.ds(base + 4, SUB, stride=2 * tiles * SUB), :] = words[1]


def inner_kernel(
    knots_ref, colour_ref, density_ref, cells, grads, bz_ref, az_ref, out_ref, sides, consts,
    *, depth_total,
):
    tiles, depth = cells.shape[:2]
    prepare(consts, knots_ref, colour_ref, density_ref, depth_total)
    for side, ref in enumerate((bz_ref, az_ref)):
        for c in range(ref.shape[0] // 16):
            plane = ref[16 * c:16 * c + 16, :].astype(jnp.float32)
            for t in range(tiles):
                for part in range(2):
                    at = slice(8 * part, 8 * part + 8)
                    sides[side, t, pl.ds(2 * c + part, SUB, stride=PITCH), :] = plane[at, lanes_of(t)]

    def tile_step(t, carry):
        def row_step(r, carry):
            at = pl.ds(PITCH * r, SUB)

            def cell(z):
                if z < 0:
                    return sides[0, t, at, :]
                if z == depth:
                    return sides[1, t, at, :]
                return cells[t, z, at, :]

            def grad_x(z):
                return cells[t, z, pl.ds(PITCH * r + PITCH, SUB), :] - cells[t, z, pl.ds(PITCH * r - PITCH, SUB), :]

            words = composite(
                consts, cell, grad_x, lambda z: grads[t, z, at, :], depth, depth_total
            )
            store_words(out_ref, words, t, r, tiles)
            return carry

        return lax.fori_loop(1, GROUPS - 1, row_step, carry, unroll=2)

    lax.fori_loop(1, tiles - 1, tile_step, 0)


def outer_kernel(
    knots_ref, colour_ref, density_ref, cells, grads, sides, x_ref, y_ref, _, out_ref, x_edges, y_edges,
    consts, *, depth_total,
):
    tiles, depth = cells.shape[:2]
    prepare(consts, knots_ref, colour_ref, density_ref, depth_total)
    gx, gy = lax.axis_index("gx"), lax.axis_index("gy")
    x_last, y_last = x_ref.shape[0] - 1, y_ref.shape[0] - 1
    x_edges[0] = jnp.where(gx > 0, x_ref[jnp.maximum(gx - 1, 0), 1].astype(jnp.float32), 0.0)
    x_edges[1] = jnp.where(gx < x_last, x_ref[jnp.minimum(gx + 1, x_last), 0].astype(jnp.float32), 0.0)
    y_edges[0] = jnp.where(gy > 0, -pltpu.roll(y_ref[jnp.maximum(gy - 1, 0)], LANES - depth, 1), 0.0)
    y_edges[1] = jnp.where(gy < y_last, y_ref[jnp.minimum(gy + 1, y_last)], 0.0)
    lane = lane_index()
    sublane = lax.broadcasted_iota(jnp.int32, (SUB, LANES), 0)

    def work(t, r, above_start, below_start):
        at = pl.ds(PITCH * r, SUB)
        edge_lane = lane == jnp.where(t == 0, 0, jnp.where(t == tiles - 1, LANES - 1, -1))
        columns = y_edges[jnp.where(t == 0, 0, 1), pl.ds(pl.multiple_of(SUB * r, SUB), SUB), :]
        at_lanes = pl.ds(pl.multiple_of(t * LANES, LANES), LANES)

        def cell(z):
            if z < 0:
                return sides[0, t, at, :]
            if z == depth:
                return sides[1, t, at, :]
            return cells[t, z, at, :]

        def grad_x(z):
            above = cells[t, z, pl.ds(above_start, SUB), :]
            below = cells[t, z, pl.ds(below_start, SUB), :]
            if isinstance(r, int) and r == 0:
                above = jnp.where(sublane == 0, x_edges[0, z:z + 1, at_lanes], above)
            if isinstance(r, int) and r == GROUPS - 1:
                below = jnp.where(sublane == SUB - 1, x_edges[1, z:z + 1, at_lanes], below)
            return below - above

        def grad_y(z):
            return grads[t, z, at, :] + jnp.where(edge_lane, columns[:, z:z + 1], 0.0)

        store_words(out_ref, composite(consts, cell, grad_x, grad_y, depth, depth_total), t, r, tiles)

    last = GROUPS - 1

    def rows_step(t, carry):
        work(t, 0, jnp.minimum(t, 0) + PITCH * last - 1, jnp.minimum(t, 0) + PITCH)
        work(t, last, jnp.minimum(t, 0) + PITCH * (last - 1), jnp.minimum(t, 0) + 1)
        return carry

    lax.fori_loop(0, tiles, rows_step, 0)

    def cols_step(r, carry):
        for t in (0, tiles - 1):
            work(t, r, PITCH * r - PITCH, PITCH * r + PITCH)
        return carry

    lax.fori_loop(1, last, cols_step, 0)


def compose_kernel(colour_ref, pieces_ref, image_ref, coverage_ref):
    count = pieces_ref.shape[0]
    low_rows = lax.broadcasted_iota(jnp.int32, (SUB, LANES), 0) < 4
    scales = [full(colour_scale(colour_ref, c)) for c in range(3)]
    step = COLOUR_SPAN / CODES
    steps_hi = jnp.where(low_rows, step, COVER_SPAN / CODES)
    start_hi = jnp.where(low_rows, -COLOUR_SPAN - step, -COVER_SPAN - COVER_SPAN / CODES)

    def decode(code, steps, start):
        value = jnp.exp2(code.astype(jnp.float32) * steps + start)
        return jnp.where(code > 0, value, 0.0)

    for t in range(pieces_ref.shape[1] // SUB):
        low = high = None
        transmit = None
        for piece in range(count):
            word = pieces_ref[piece, t * SUB:(t + 1) * SUB, :]
            red_blue = decode(word & 0xFFFF, step, -COLOUR_SPAN - step)
            green_cover = decode(lax.shift_right_logical(word, 16), steps_hi, start_hi)
            cover = jnp.where(low_rows, pltpu.roll(green_cover, 4, 0), green_cover)
            if piece == 0:
                low, high, transmit = red_blue, green_cover, 1.0 - cover
            else:
                low = low + transmit * red_blue
                high = high + transmit * green_cover
                transmit = transmit * (1.0 - cover)
        low = low * jnp.where(low_rows, scales[0], scales[2])
        high = high * jnp.where(low_rows, scales[1], 1.0)
        image_ref[0, :, lanes_of(t)] = low[:4]
        image_ref[1, :, lanes_of(t)] = high[:4]
        image_ref[2, :, lanes_of(t)] = low[4:]
        coverage_ref[:, lanes_of(t)] = high[4:]


def cost(flops, moved):
    return pl.CostEstimate(flops=flops, bytes_accessed=moved, transcendentals=0)


def on_device(volume, knot_bins, tf_colour, tf_density):
    depth, rows, cols = volume.shape
    count = lax.axis_size("gz")
    tiles = cols // LANES
    depth_total = float(depth * count)
    smem = pl.BlockSpec(memory_space=pltpu.SMEM)
    vmem = pl.BlockSpec(memory_space=pltpu.VMEM)
    params = pltpu.CompilerParams(vmem_limit_bytes=24 << 20)
    f32 = jnp.float32

    def whole(*shape):
        return pl.BlockSpec(shape, lambda n: (0,) * len(shape))

    x_edges, y_edges, front, rear = pl.pallas_call(
        edges_kernel,
        grid=(1,),
        out_shape=(
            jax.ShapeDtypeStruct((2, depth, cols), volume.dtype),
            jax.ShapeDtypeStruct((rows, LANES), f32),
            jax.ShapeDtypeStruct((rows, cols), volume.dtype),
            jax.ShapeDtypeStruct((rows, cols), volume.dtype),
        ),
        in_specs=[
            pl.BlockSpec((depth, 16, cols), lambda n: (0, 0, 0)),
            pl.BlockSpec((depth, 16, cols), lambda n: (0, rows // 16 - 1, 0)),
            pl.BlockSpec((depth, rows, LANES), lambda n: (0, 0, 0)),
            pl.BlockSpec((depth, rows, LANES), lambda n: (0, 0, tiles - 1)),
            pl.BlockSpec((1, rows, cols), lambda n: (0, 0, 0)),
            pl.BlockSpec((1, rows, cols), lambda n: (depth - 1, 0, 0)),
        ],
        out_specs=(whole(2, depth, cols), whole(rows, LANES), whole(rows, cols), whole(rows, cols)),
        scratch_shapes=[pltpu.VMEM((2, depth, cols), f32)],
        compiler_params=params,
        cost_estimate=cost(1 << 20, 2 << 20),
        name="edges",
    )(*[volume] * 6)
    x_all = lax.all_gather(x_edges, "gx")
    y_all = lax.all_gather(y_edges, "gy")
    up = [(i, i + 1) for i in range(count - 1)]
    down = [(j, i) for i, j in up]
    bz = lax.ppermute(rear, "gz", up)
    az = lax.ppermute(front, "gz", down)

    cells, grads = pl.pallas_call(
        spread_kernel,
        out_shape=(
            jax.ShapeDtypeStruct((tiles, depth, PITCH * GROUPS, LANES), f32),
            jax.ShapeDtypeStruct((tiles, depth, PITCH * GROUPS, LANES), f32),
        ),
        in_specs=[vmem],
        out_specs=(vmem, vmem),
        compiler_params=params,
        cost_estimate=cost(1 << 23, 2 << 20),
        name="spread",
    )(volume)

    tables = (knot_bins, tf_colour, tf_density)
    words = jax.ShapeDtypeStruct((count * tiles * SUB, LANES), jnp.int32)
    side_shape = (2, tiles, PITCH * GROUPS, LANES)
    inner, sides = pl.pallas_call(
        functools.partial(inner_kernel, depth_total=depth_total),
        out_shape=(words, jax.ShapeDtypeStruct(side_shape, f32)),
        in_specs=[smem] * 3 + [vmem] * 4,
        out_specs=(vmem, vmem),
        scratch_shapes=[pltpu.VMEM((40, SUB, LANES), f32)],
        compiler_params=params,
        cost_estimate=cost(1 << 26, 1 << 23),
        name="inner",
    )(*tables, cells, grads, bz, az)
    codes = pl.pallas_call(
        functools.partial(outer_kernel, depth_total=depth_total),
        out_shape=words,
        in_specs=[smem] * 3 + [vmem] * 6,
        out_specs=vmem,
        input_output_aliases={8: 0},
        scratch_shapes=[
            pltpu.VMEM((2, depth, cols), f32),
            pltpu.VMEM((2, rows, LANES), f32),
            pltpu.VMEM((40, SUB, LANES), f32),
        ],
        compiler_params=params,
        cost_estimate=cost(1 << 26, 1 << 23),
        name="outer",
    )(*tables, cells, grads, sides, x_all, y_all, inner)
    pieces = lax.all_to_all(
        codes.reshape(count, tiles * SUB, LANES), "gz", split_axis=0, concat_axis=0, tiled=True
    )
    band = rows // count
    return pl.pallas_call(
        compose_kernel,
        out_shape=(
            jax.ShapeDtypeStruct((3, band, cols), f32),
            jax.ShapeDtypeStruct((band, cols), f32),
        ),
        in_specs=[smem, vmem],
        out_specs=(vmem, vmem),
        name="compose",
    )(tf_colour, pieces)


def solution(mesh):
    placed = (P("gz", "gx", "gy"), P(), P(), P())
    return jax.shard_map(
        on_device,
        mesh=mesh,
        in_specs=placed,
        out_specs=(P(None, ("gx", "gz"), "gy"), P(("gx", "gz"), "gy")),
        check_vma=False,
    )
```

```python
import functools
import math

import jax
import jax.numpy as jnp
import numpy as np
from jax import lax
from jax.experimental import pallas as pl
from jax.experimental.pallas import tpu as pltpu
from jax.sharding import PartitionSpec as P

BINS = 256
KNOTS = 8
SEGMENTS = KNOTS - 1
AMBIENT = 0.2
LANES = 128
SUB = 8
GROUPS = 8
PITCH = 9

COLOUR_SPAN = 26.0
COVER_SPAN = 9.0
CODES = 65534.0


def colour_scale(colour_ref, channel):
    largest = colour_ref[channel, 0]
    for k in range(1, KNOTS):
        largest = jnp.maximum(largest, colour_ref[channel, k])
    return jnp.maximum(largest, 1e-30)


def encode(value, span):
    position = (jnp.log2(jnp.maximum(value, 2.0 ** (-span - 1.0))) + span) * (CODES / span) + 1.5
    return jnp.clip(position, 0.0, 65535.0).astype(jnp.int32)


def opacity_terms(largest):
    half = 0.5 * largest
    nodes = [half + half * math.cos(math.pi * (2 * i + 1) / 8.0) for i in range(4)]
    values = [-math.expm1(-y) / y for y in nodes]
    return [float(c) for c in np.polynomial.polynomial.polyfit(nodes, values, 3)]


def full(x):
    return jnp.full((SUB, LANES), x, jnp.float32)


def lanes_of(t):
    return slice(t * LANES, (t + 1) * LANES)


def lane_index():
    return lax.broadcasted_iota(jnp.int32, (SUB, LANES), 1)


def edges_kernel(x_low, x_high, y_low, y_high, z_low, z_high, top, bottom, y_out, front, rear, rows_x):
    depth = x_low.shape[0]
    cols = x_low.shape[2]
    for z in range(depth):
        low = x_low[z].astype(jnp.float32)
        high = x_high[z].astype(jnp.float32)
        rows_x[0, z:z + 1, :] = low[:1]
        rows_x[1, z:z + 1, :] = high[15:]
    top[...] = rows_x[0].astype(top.dtype)
    bottom[...] = rows_x[1].astype(bottom.dtype)
    lane = lane_index()
    for i in range(GROUPS // 2):
        sides = [jnp.zeros((SUB, LANES), jnp.float32)] * 2
        for z in range(depth):
            low = y_low[z, 16 * i:16 * i + 16, :].astype(jnp.float32)
            high = y_high[z, 16 * i:16 * i + 16, :].astype(jnp.float32)
            for part in range(2):
                at = slice(8 * part, 8 * part + 8)
                sides[part] = jnp.where(lane == z, low[at, :1], sides[part])
                sides[part] = jnp.where(lane == depth + z, high[at, LANES - 1:], sides[part])
        for part in range(2):
            y_out[pl.ds(2 * i + part, SUB, stride=GROUPS), :] = sides[part]
    front[...] = z_low[0]
    rear[...] = z_high[0]


def spread_kernel(vol_ref, cells, grads):
    depth, rows, cols = vol_ref.shape
    lane = lax.broadcasted_iota(jnp.int32, (16, LANES), 1)
    tiles = cols // LANES

    def step(z, carry):
        for c in range(rows // 16):
            plane = vol_ref[z, 16 * c:16 * c + 16, :].astype(jnp.float32)
            left = pltpu.roll(plane, 1, 1)
            right = pltpu.roll(plane, cols - 1, 1)
            for t in range(tiles):
                l, r = left[:, lanes_of(t)], right[:, lanes_of(t)]
                if t == 0:
                    l = jnp.where(lane == 0, 0.0, l)
                if t == tiles - 1:
                    r = jnp.where(lane == LANES - 1, 0.0, r)
                across = r - l
                own = plane[:, lanes_of(t)]
                for part in range(2):
                    i = 2 * c + part
                    at = slice(8 * part, 8 * part + 8)
                    cells[t, z, pl.ds(i, SUB, stride=PITCH), :] = own[at]
                    grads[t, z, pl.ds(i, SUB, stride=PITCH), :] = across[at]
        return carry

    lax.fori_loop(0, depth, step, 0)


def prepare(consts, knots_ref, colour_ref, density_ref, depth_total):
    top = BINS - 1.0
    spans = []
    for k in range(SEGMENTS):
        low = full(knots_ref[k].astype(jnp.float32))
        high = full(knots_ref[k + 1].astype(jnp.float32))
        spans.append((high - low) * (1.0 / top))
        if k:
            consts[k - 1] = low / top
    consts[6] = full(density_ref[0]) * (1.0 / depth_total)
    for k in range(SEGMENTS):
        step = full(density_ref[k + 1]) - full(density_ref[k])
        consts[7 + k] = step * (1.0 / depth_total) / spans[k]
    for c in range(3):
        scale = full(colour_scale(colour_ref, c))
        consts[14 + 8 * c] = full(colour_ref[c, 0]) / scale
        for k in range(SEGMENTS):
            step = full(colour_ref[c, k + 1]) - full(colour_ref[c, k])
            consts[15 + 8 * c + k] = step / scale / spans[k]


def composite(consts, cell, grad_x, grad_y, depth, depth_total):
    c0, c1, c2, c3 = opacity_terms(10.0 / depth_total)
    points = [consts[k] for k in range(6)]
    first = consts[6]
    slopes = [consts[7 + k] for k in range(SEGMENTS)]
    transmit = jnp.ones((SUB, LANES), jnp.float32)
    weight = None
    moments = None
    earlier, now = cell(-1), cell(0)
    for z in range(depth):
        later = cell(z + 1)
        gx, gy, gz = grad_x(z), grad_y(z), later - earlier
        across = gy + gz
        facing = jnp.abs(gx + (across + across))
        shading = AMBIENT + facing * (
            ((1.0 - AMBIENT) / 3.0) * lax.rsqrt(gx * gx + gy * gy + (gz * gz + 1.0))
        )
        capped = [jnp.minimum(now, p) for p in points] + [now]
        ramps = [capped[0]] + [capped[k + 1] - capped[k] for k in range(6)]
        y = first
        for k in range(SEGMENTS):
            y = y + ramps[k] * slopes[k]
        taken = transmit * (y * (c0 + y * (c1 + y * (c2 + y * c3))))
        transmit = transmit - taken
        shaded = taken * shading
        if z == 0:
            weight = shaded
            moments = [shaded * r for r in ramps]
        else:
            weight = weight + shaded
            moments = [m + shaded * r for m, r in zip(moments, ramps)]
        earlier, now = now, later
    values = []
    for c in range(3):
        value = weight * consts[14 + 8 * c]
        for k in range(SEGMENTS):
            value = value + moments[k] * consts[15 + 8 * c + k]
        values.append(value)
    return values + [1.0 - transmit]


def spread_side(ref, sides, side):
    for c in range(ref.shape[0] // 16):
        plane = ref[16 * c:16 * c + 16, :].astype(jnp.float32)
        for t in range(sides.shape[1]):
            for part in range(2):
                own = plane[8 * part:8 * part + 8, lanes_of(t)]
                sides[side, t, pl.ds(2 * c + part, SUB, stride=PITCH), :] = own


def place_edges(cells, grads, bx_ref, ax_ref, by_ref, ay_ref):
    tiles, depth = cells.shape[:2]
    for slot, ref in ((PITCH * (GROUPS - 1) - 1, bx_ref), (GROUPS, ax_ref)):
        edge = ref[...].astype(jnp.float32)
        for z in range(depth):
            for t in range(tiles):
                cells[t, z, slot:slot + 1, :] = edge[z:z + 1, lanes_of(t)]
    lane = lane_index()

    def step(r, carry):
        rows = pl.ds(pl.multiple_of(SUB * r, SUB), SUB)
        at = pl.ds(PITCH * r, SUB)
        before, after = by_ref[rows, :], ay_ref[rows, :]
        for z in range(depth):
            first = jnp.where(lane == 0, before[:, depth + z:depth + z + 1], 0.0)
            last = jnp.where(lane == LANES - 1, after[:, z:z + 1], 0.0)
            grads[0, z, at, :] = grads[0, z, at, :] - first
            grads[tiles - 1, z, at, :] = grads[tiles - 1, z, at, :] + last
        return carry

    lax.fori_loop(0, GROUPS, step, 0)


def half_loop(consts, cells, grads, sides, parity, depth_total, store):
    tiles, depth = cells.shape[:2]

    def tile_step(t, carry):
        def row_step(j, carry):
            r = 4 * parity + j
            at = pl.ds(PITCH * r, SUB)
            above = pl.ds(jnp.where(r == 0, PITCH * (GROUPS - 1) - 1, PITCH * r - PITCH), SUB)
            below = pl.ds(jnp.where(r == GROUPS - 1, 1, PITCH * r + PITCH), SUB)

            def cell(z):
                if z < 0:
                    return sides[0, t, at, :]
                if z == depth:
                    return sides[1, t, at, :]
                return cells[t, z, at, :]

            values = composite(
                consts,
                cell,
                lambda z: cells[t, z, below, :] - cells[t, z, above, :],
                lambda z: grads[t, z, at, :],
                depth,
                depth_total,
            )
            store(t, j, values)
            return carry

        return lax.fori_loop(0, 4, row_step, carry, unroll=2)

    lax.fori_loop(0, tiles, tile_step, 0)


def pack(values):
    codes = [encode(v, COLOUR_SPAN) for v in values[:3]] + [encode(values[3], COVER_SPAN)]
    return codes[0] | (codes[1] << 16), codes[2] | (codes[3] << 16)


def decode(code, span):
    value = jnp.exp2(code.astype(jnp.float32) * (span / CODES) - (span + span / CODES))
    return jnp.where(code > 0, value, 0.0)


def theirs_kernel(
    knots_ref, colour_ref, density_ref, cells_in, grads_in, bx_ref, ax_ref, by_ref, ay_ref, bz_ref, az_ref,
    out_ref, cells, grads, sides, consts, *, depth_total,
):
    prepare(consts, knots_ref, colour_ref, density_ref, depth_total)
    spread_side(bz_ref, sides, 0)
    spread_side(az_ref, sides, 1)
    place_edges(cells, grads, bx_ref, ax_ref, by_ref, ay_ref)

    def store(t, j, values):
        first, second = pack(values)
        out_ref[j, t] = first
        out_ref[4 + j, t] = second

    parity = 1 - lax.rem(lax.axis_index("gz"), 2)
    half_loop(consts, cells, grads, sides, parity, depth_total, store)


def ours_kernel(
    knots_ref, colour_ref, density_ref, cells, grads, sides, out_ref, consts, *, depth_total,
):
    prepare(consts, knots_ref, colour_ref, density_ref, depth_total)

    def store(t, j, values):
        for c in range(4):
            out_ref[4 * c + j, t] = values[c]

    parity = lax.rem(lax.axis_index("gz"), 2)
    half_loop(consts, cells, grads, sides, parity, depth_total, store)


def pair_kernel(ours_ref, theirs_ref, out_ref):
    tiles = ours_ref.shape[1]
    front = lax.rem(lax.axis_index("gz"), 2) == 0

    def step(t, carry):
        for j in range(4):
            ours = [ours_ref[4 * c + j, t] for c in range(4)]
            first, second = theirs_ref[j, t], theirs_ref[4 + j, t]
            theirs = [
                decode(first & 0xFFFF, COLOUR_SPAN),
                decode(lax.shift_right_logical(first, 16), COLOUR_SPAN),
                decode(second & 0xFFFF, COLOUR_SPAN),
                decode(lax.shift_right_logical(second, 16), COVER_SPAN),
            ]
            keep_ours = jnp.where(front, 1.0, 1.0 - theirs[3])
            keep_theirs = jnp.where(front, 1.0 - ours[3], 1.0)
            words = pack([o * keep_ours + p * keep_theirs for o, p in zip(ours, theirs)])
            for w in range(2):
                out_ref[pl.ds(t * SUB + 4 * w + j, SUB, stride=tiles * SUB), :] = words[w]
        return carry

    lax.fori_loop(0, tiles, step, 0)


def compose_kernel(colour_ref, pieces_ref, image_ref, coverage_ref):
    count = pieces_ref.shape[0]
    low_rows = lax.broadcasted_iota(jnp.int32, (SUB, LANES), 0) < 4
    scales = [full(colour_scale(colour_ref, c)) for c in range(3)]
    step = COLOUR_SPAN / CODES
    steps_hi = jnp.where(low_rows, step, COVER_SPAN / CODES)
    start_hi = jnp.where(low_rows, -COLOUR_SPAN - step, -COVER_SPAN - COVER_SPAN / CODES)

    def level(code, steps, start):
        value = jnp.exp2(code.astype(jnp.float32) * steps + start)
        return jnp.where(code > 0, value, 0.0)

    for t in range(pieces_ref.shape[1] // SUB):
        low = high = None
        transmit = None
        for piece in range(count):
            word = pieces_ref[piece, t * SUB:(t + 1) * SUB, :]
            red_blue = level(word & 0xFFFF, step, -COLOUR_SPAN - step)
            green_cover = level(lax.shift_right_logical(word, 16), steps_hi, start_hi)
            cover = jnp.where(low_rows, pltpu.roll(green_cover, 4, 0), green_cover)
            if piece == 0:
                low, high, transmit = red_blue, green_cover, 1.0 - cover
            else:
                low = low + transmit * red_blue
                high = high + transmit * green_cover
                transmit = transmit * (1.0 - cover)
        low = low * jnp.where(low_rows, scales[0], scales[2])
        high = high * jnp.where(low_rows, scales[1], 1.0)
        image_ref[0, :, lanes_of(t)] = low[:4]
        image_ref[1, :, lanes_of(t)] = high[:4]
        image_ref[2, :, lanes_of(t)] = low[4:]
        coverage_ref[:, lanes_of(t)] = high[4:]


def neighbours(last, initial, axis):
    count = lax.axis_size(axis)
    up = [(i, i + 1) for i in range(count - 1)]
    down = [(j, i) for i, j in up]
    return lax.ppermute(last, axis, up), lax.ppermute(initial, axis, down)


def cost(flops, moved):
    return pl.CostEstimate(flops=flops, bytes_accessed=moved, transcendentals=0)


def on_device(volume, knot_bins, tf_colour, tf_density):
    depth, rows, cols = volume.shape
    count = lax.axis_size("gz")
    tiles = cols // LANES
    depth_total = float(depth * count)
    smem = pl.BlockSpec(memory_space=pltpu.SMEM)
    vmem = pl.BlockSpec(memory_space=pltpu.VMEM)
    params = pltpu.CompilerParams(vmem_limit_bytes=24 << 20)
    f32 = jnp.float32

    def whole(*shape):
        return pl.BlockSpec(shape, lambda n: (0,) * len(shape))

    top, bottom, y_edges, front, rear = pl.pallas_call(
        edges_kernel,
        grid=(1,),
        out_shape=(
            jax.ShapeDtypeStruct((depth, cols), volume.dtype),
            jax.ShapeDtypeStruct((depth, cols), volume.dtype),
            jax.ShapeDtypeStruct((rows, LANES), f32),
            jax.ShapeDtypeStruct((rows, cols), volume.dtype),
            jax.ShapeDtypeStruct((rows, cols), volume.dtype),
        ),
        in_specs=[
            pl.BlockSpec((depth, 16, cols), lambda n: (0, 0, 0)),
            pl.BlockSpec((depth, 16, cols), lambda n: (0, rows // 16 - 1, 0)),
            pl.BlockSpec((depth, rows, LANES), lambda n: (0, 0, 0)),
            pl.BlockSpec((depth, rows, LANES), lambda n: (0, 0, tiles - 1)),
            pl.BlockSpec((1, rows, cols), lambda n: (0, 0, 0)),
            pl.BlockSpec((1, rows, cols), lambda n: (depth - 1, 0, 0)),
        ],
        out_specs=(whole(depth, cols), whole(depth, cols), whole(rows, LANES), whole(rows, cols), whole(rows, cols)),
        scratch_shapes=[pltpu.VMEM((2, depth, cols), f32)],
        compiler_params=params,
        cost_estimate=cost(1 << 20, 2 << 20),
        name="edges",
    )(*[volume] * 6)
    bz, az = neighbours(rear, front, "gz")
    by, ay = neighbours(y_edges, y_edges, "gy")
    bx, ax = neighbours(bottom, top, "gx")
    spread_shape = jax.ShapeDtypeStruct((tiles, depth, PITCH * GROUPS, LANES), f32)
    cells, grads = pl.pallas_call(
        spread_kernel,
        out_shape=(spread_shape, spread_shape),
        in_specs=[vmem],
        out_specs=(vmem, vmem),
        compiler_params=params,
        cost_estimate=cost(1 << 23, 2 << 20),
        name="spread",
    )(volume)
    tables = (knot_bins, tf_colour, tf_density)
    consts = [pltpu.VMEM((40, SUB, LANES), f32)]
    theirs, cells, grads, sides = pl.pallas_call(
        functools.partial(theirs_kernel, depth_total=depth_total),
        out_shape=(
            jax.ShapeDtypeStruct((8, tiles, SUB, LANES), jnp.int32),
            spread_shape,
            spread_shape,
            jax.ShapeDtypeStruct((2, tiles, PITCH * GROUPS, LANES), f32),
        ),
        in_specs=[smem] * 3 + [vmem] * 8,
        out_specs=(vmem,) * 4,
        input_output_aliases={3: 1, 4: 2},
        scratch_shapes=consts,
        compiler_params=params,
        cost_estimate=cost(1 << 26, 1 << 23),
        name="theirs",
    )(*tables, cells, grads, bx, ax, by, ay, bz, az)
    pairs = [(i, i ^ 1) for i in range(count)]
    arrived = lax.ppermute(theirs, "gz", pairs)
    ours = pl.pallas_call(
        functools.partial(ours_kernel, depth_total=depth_total),
        out_shape=jax.ShapeDtypeStruct((16, tiles, SUB, LANES), f32),
        in_specs=[smem] * 3 + [vmem] * 3,
        out_specs=vmem,
        scratch_shapes=consts,
        compiler_params=params,
        cost_estimate=cost(1 << 26, 1 << 23),
        name="ours",
    )(*tables, cells, grads, sides)
    half = count // 2
    codes = pl.pallas_call(
        pair_kernel,
        out_shape=jax.ShapeDtypeStruct((half * tiles * SUB, LANES), jnp.int32),
        in_specs=[vmem] * 2,
        out_specs=vmem,
        compiler_params=params,
        name="pair",
    )(ours, arrived)
    pieces = lax.all_to_all(
        codes.reshape(half, tiles * SUB, LANES),
        "gz",
        split_axis=0,
        concat_axis=0,
        tiled=True,
        axis_index_groups=[[2 * i + e for i in range(half)] for e in range(2)],
    )
    band = rows // count
    return pl.pallas_call(
        compose_kernel,
        out_shape=(
            jax.ShapeDtypeStruct((3, band, cols), f32),
            jax.ShapeDtypeStruct((band, cols), f32),
        ),
        in_specs=[smem, vmem],
        out_specs=(vmem, vmem),
        name="compose",
    )(tf_colour, pieces)


def solution(mesh):
    placed = (P("gz", "gx", "gy"), P(), P(), P())
    return jax.shard_map(
        on_device,
        mesh=mesh,
        in_specs=placed,
        out_specs=(P(None, ("gx", "gz"), "gy"), P(("gx", "gz"), "gy")),
        check_vma=False,
    )
```

```python
import functools
import math

import jax
import jax.numpy as jnp
import numpy as np
from jax import lax
from jax.experimental import pallas as pl
from jax.experimental.pallas import tpu as pltpu
from jax.sharding import PartitionSpec as P

BINS = 256
KNOTS = 8
SEGMENTS = KNOTS - 1
AMBIENT = 0.2
LANES = 128
SUB = 8
QUAD = 4
STEP = 4
MARGIN = 4
SCALES = 38

COLOUR_SPAN = 26.0
COVER_SPAN = 9.0
CODES = 65534.0


def colour_scale(colour_ref, channel):
    largest = colour_ref[channel, 0]
    for k in range(1, KNOTS):
        largest = jnp.maximum(largest, colour_ref[channel, k])
    return jnp.maximum(largest, 1e-30)


def encode(value, span):
    position = (jnp.log2(jnp.maximum(value, 2.0 ** (-span - 1.0))) + span) * (CODES / span) + 1.5
    return jnp.clip(position, 0.0, 65535.0).astype(jnp.int32)


def opacity_terms(largest):
    half = 0.5 * largest
    nodes = [half + half * math.cos(math.pi * (2 * i + 1) / 6.0) for i in range(3)]
    values = [-math.expm1(-y) / y for y in nodes]
    c0, c1, c2 = (float(c) for c in np.polynomial.polynomial.polyfit(nodes, values, 2))
    k = c2 ** (1.0 / 3.0)
    a = c1 / (2.0 * k * k)
    return k, a, c0 / k - a * a


def full(x):
    return jnp.full((SUB, LANES), x, jnp.float32)


def lanes_of(t):
    return slice(t * LANES, (t + 1) * LANES)


def lane_index():
    return lax.broadcasted_iota(jnp.int32, (SUB, LANES), 1)


def edges_kernel(x_low, x_high, y_low, y_high, z_low, z_high, top, bottom, y_out, front, rear, rows_x):
    depth = x_low.shape[0]
    cols = x_low.shape[2]
    for z in range(depth):
        low = x_low[z].astype(jnp.float32)
        high = x_high[z].astype(jnp.float32)
        rows_x[0, z:z + 1, :] = low[:1]
        rows_x[1, z:z + 1, :] = high[15:]
    top[...] = rows_x[0].astype(top.dtype)
    bottom[...] = rows_x[1].astype(bottom.dtype)
    lane = lane_index()
    for i in range(y_low.shape[1] // 16):
        sides = [jnp.zeros((SUB, LANES), jnp.float32)] * 2
        for z in range(depth):
            low = y_low[z, 16 * i:16 * i + 16, :].astype(jnp.float32)
            high = y_high[z, 16 * i:16 * i + 16, :].astype(jnp.float32)
            for part in range(2):
                at = slice(8 * part, 8 * part + 8)
                sides[part] = jnp.where(lane == z, low[at, :1], sides[part])
                sides[part] = jnp.where(lane == depth + z, high[at, LANES - 1:], sides[part])
        for part in range(2):
            y_out[pl.ds(SUB * STEP * part + i, SUB, stride=STEP), :] = sides[part]
    front[...] = z_low[0]
    rear[...] = z_high[0]


def slots_of(i):
    return pl.ds(MARGIN + SUB * STEP * (i % 2) + i // 2, SUB, stride=STEP)


def spread_kernel(knots_ref, colour_ref, density_ref, vol_ref, cells, grads, consts, *, depth_total):
    depth, rows, cols = vol_ref.shape
    lane = lax.broadcasted_iota(jnp.int32, (16, LANES), 1)
    tiles = cols // LANES
    prepare(consts, knots_ref, colour_ref, density_ref, depth_total)

    def step(z, carry):
        for c in range(rows // 16):
            plane = vol_ref[z, 16 * c:16 * c + 16, :].astype(jnp.float32)
            left = pltpu.roll(plane, 1, 1)
            right = pltpu.roll(plane, cols - 1, 1)
            for t in range(tiles):
                l, r = left[:, lanes_of(t)], right[:, lanes_of(t)]
                if t == 0:
                    l = jnp.where(lane == 0, 0.0, l)
                if t == tiles - 1:
                    r = jnp.where(lane == LANES - 1, 0.0, r)
                across = r - l
                own = plane[:, lanes_of(t)]
                for part in range(2):
                    at = slice(8 * part, 8 * part + 8)
                    cells[t, z, slots_of(2 * c + part), :] = own[at]
                    grads[t, z, slots_of(2 * c + part), :] = across[at]
                if c:
                    slot = MARGIN + rows + c - 1
                    cells[t, z, slot:slot + 1, :] = own[:1]
                if c < rows // 16 - 1:
                    cells[t, z, c + 1:c + 2, :] = own[15:]
        return carry

    lax.fori_loop(0, depth, step, 0)


def prepare(consts, knots_ref, colour_ref, density_ref, depth_total):
    top = BINS - 1.0
    spans = []
    for k in range(SEGMENTS):
        low = full(knots_ref[k].astype(jnp.float32))
        high = full(knots_ref[k + 1].astype(jnp.float32))
        spans.append((high - low) * (1.0 / top))
        if k:
            consts[k - 1] = low / top
    unit = opacity_terms(10.0 / depth_total)[0] / depth_total
    consts[6] = full(density_ref[0]) * unit
    for k in range(SEGMENTS):
        step = full(density_ref[k + 1]) - full(density_ref[k])
        consts[7 + k] = step * unit / spans[k]
    for c in range(3):
        scale = full(colour_scale(colour_ref, c))
        consts[SCALES + c] = scale
        consts[14 + 8 * c] = full(colour_ref[c, 0]) / scale
        for k in range(SEGMENTS):
            step = full(colour_ref[c, k + 1]) - full(colour_ref[c, k])
            consts[15 + 8 * c + k] = step / scale / spans[k]


def composite(consts, cell, grad_x, grad_y, depth, depth_total):
    _, shift, rest = opacity_terms(10.0 / depth_total)
    points = [consts[k] for k in range(6)]
    first = consts[6]
    slopes = [consts[7 + k] for k in range(SEGMENTS)]
    transmit = jnp.ones((SUB, LANES), jnp.float32)
    weight = None
    moments = None
    earlier, now = cell(-1), cell(0)
    for z in range(depth):
        later = cell(z + 1)
        gx, gy, gz = grad_x(z), grad_y(z), later - earlier
        across = gy + gz
        facing = jnp.abs(gx + (across + across))
        shading = AMBIENT + facing * (
            ((1.0 - AMBIENT) / 3.0) * lax.rsqrt(gx * gx + gy * gy + (gz * gz + 1.0))
        )
        capped = [jnp.minimum(now, p) for p in points] + [now]
        ramps = [capped[0]] + [capped[k + 1] - capped[k] for k in range(6)]
        y = first
        for k in range(SEGMENTS):
            y = y + ramps[k] * slopes[k]
        shifted = y + shift
        taken = transmit * (y * (shifted * shifted + rest))
        transmit = transmit - taken
        shaded = taken * shading
        if z == 0:
            weight = shaded
            moments = [shaded * r for r in ramps]
        else:
            weight = weight + shaded
            moments = [m + shaded * r for m, r in zip(moments, ramps)]
        earlier, now = now, later
    values = []
    for c in range(3):
        value = weight * consts[14 + 8 * c]
        for k in range(SEGMENTS):
            value = value + moments[k] * consts[15 + 8 * c + k]
        values.append(value)
    return values + [1.0 - transmit]


def spread_side(ref, sides, side):
    for c in range(ref.shape[0] // 16):
        plane = ref[16 * c:16 * c + 16, :].astype(jnp.float32)
        for t in range(sides.shape[1]):
            for part in range(2):
                sides[side, t, slots_of(2 * c + part), :] = plane[8 * part:8 * part + 8, lanes_of(t)]


def place_edges(cells, grads, bx_ref, ax_ref, by_ref, ay_ref):
    tiles, depth, slots = cells.shape[:3]
    for slot, ref in ((0, bx_ref), (slots - 1, ax_ref)):
        edge = ref[...].astype(jnp.float32)
        for z in range(depth):
            for t in range(tiles):
                cells[t, z, slot:slot + 1, :] = edge[z:z + 1, lanes_of(t)]
    lane = lane_index()

    def step(g, carry):
        rows = pl.ds(pl.multiple_of(SUB * g, SUB), SUB)
        at = pl.ds(SUB * g + MARGIN, SUB)
        before, after = by_ref[rows, :], ay_ref[rows, :]
        for z in range(depth):
            first = jnp.where(lane == 0, before[:, depth + z:depth + z + 1], 0.0)
            last = jnp.where(lane == LANES - 1, after[:, z:z + 1], 0.0)
            grads[0, z, at, :] = grads[0, z, at, :] - first
            grads[tiles - 1, z, at, :] = grads[tiles - 1, z, at, :] + last
        return carry

    lax.fori_loop(0, by_ref.shape[0] // SUB, step, 0)


def quarter_loop(consts, cells, grads, sides, owner, depth_total, store):
    tiles, depth = cells.shape[:2]

    def step(t, carry):
        for p in range(2):
            start = MARGIN + STEP * (4 * owner + 2 * p)
            at, above, below = (pl.ds(start + shift, SUB) for shift in (0, -STEP, STEP))

            def cell(z):
                if z < 0:
                    return sides[0, t, at, :]
                if z == depth:
                    return sides[1, t, at, :]
                return cells[t, z, at, :]

            values = composite(
                consts,
                cell,
                lambda z: cells[t, z, below, :] - cells[t, z, above, :],
                lambda z: grads[t, z, at, :],
                depth,
                depth_total,
            )
            store(t, p, values)
        return carry

    lax.fori_loop(0, tiles, step, 0)


def pack(values):
    codes = [encode(v, COLOUR_SPAN) for v in values[:3]] + [encode(values[3], COVER_SPAN)]
    return codes[0] | (codes[1] << 16), codes[2] | (codes[3] << 16)


def decode(code, span):
    value = jnp.exp2(code.astype(jnp.float32) * (span / CODES) - (span + span / CODES))
    return jnp.where(code > 0, value, 0.0)


def place_in_quad():
    return lax.rem(lax.axis_index("gz"), QUAD)


def send_quarter(consts, cells, grads, sides, out_ref, mate, depth_total):
    def store(t, p, values):
        first, second = pack(values)
        out_ref[p, t] = first
        out_ref[2 + p, t] = second

    quarter_loop(consts, cells, grads, sides, place_in_quad() ^ mate, depth_total, store)


def first_kernel(
    consts, cells_in, grads_in, bx_ref, ax_ref, by_ref, ay_ref, bz_ref, az_ref,
    out_ref, cells, grads, sides, *, mate, depth_total,
):
    spread_side(bz_ref, sides, 0)
    spread_side(az_ref, sides, 1)
    place_edges(cells, grads, bx_ref, ax_ref, by_ref, ay_ref)
    send_quarter(consts, cells, grads, sides, out_ref, mate, depth_total)


def later_kernel(consts, cells, grads, sides, _, out_ref, *, mate, depth_total):
    send_quarter(consts, cells, grads, sides, out_ref, mate, depth_total)


def ours_kernel(consts, cells, grads, sides, _, out_ref, *, depth_total):
    def store(t, p, values):
        for c in range(4):
            out_ref[2 * c + p, t] = values[c]

    quarter_loop(consts, cells, grads, sides, place_in_quad(), depth_total, store)


def quad_kernel(ours_ref, mate1_ref, mate2_ref, mate3_ref, out_ref):
    tiles = ours_ref.shape[1]
    mates = (ours_ref, mate1_ref, mate2_ref, mate3_ref)

    def piece(k, t, p):
        if k == 0:
            return [ours_ref[2 * c + p, t] for c in range(4)]
        first, second = mates[k][p, t], mates[k][2 + p, t]
        return [
            decode(first & 0xFFFF, COLOUR_SPAN),
            decode(lax.shift_right_logical(first, 16), COLOUR_SPAN),
            decode(second & 0xFFFF, COLOUR_SPAN),
            decode(lax.shift_right_logical(second, 16), COVER_SPAN),
        ]

    for place in range(QUAD):

        @pl.when(place_in_quad() == place)
        def _():
            def step(t, carry):
                for p in range(2):
                    total = piece(place, t, p)
                    for other in range(1, QUAD):
                        rear = piece(place ^ other, t, p)
                        keep = 1.0 - total[3]
                        total = [a + keep * b for a, b in zip(total, rear)]
                    for w, word in enumerate(pack(total)):
                        for q in range(2):
                            row = t * SUB + 4 * w + 2 * p + q
                            out_ref[pl.ds(row, 4, stride=tiles * SUB), :] = word[4 * q:4 * q + 4]
                return carry

            lax.fori_loop(0, tiles, step, 0)


def compose_kernel(consts, pieces_ref, image_ref, coverage_ref):
    count = pieces_ref.shape[0]
    low_rows = lax.broadcasted_iota(jnp.int32, (SUB, LANES), 0) < 4
    scales = [consts[SCALES + c] for c in range(3)]
    step = COLOUR_SPAN / CODES
    steps_hi = jnp.where(low_rows, step, COVER_SPAN / CODES)
    start_hi = jnp.where(low_rows, -COLOUR_SPAN - step, -COVER_SPAN - COVER_SPAN / CODES)

    def level(code, steps, start):
        value = jnp.exp2(code.astype(jnp.float32) * steps + start)
        return jnp.where(code > 0, value, 0.0)

    for t in range(pieces_ref.shape[1] // SUB):
        low = high = None
        transmit = None
        for piece in range(count):
            word = pieces_ref[piece, t * SUB:(t + 1) * SUB, :]
            red_blue = level(word & 0xFFFF, step, -COLOUR_SPAN - step)
            green_cover = level(lax.shift_right_logical(word, 16), steps_hi, start_hi)
            cover = jnp.where(low_rows, pltpu.roll(green_cover, 4, 0), green_cover)
            if piece == 0:
                low, high, transmit = red_blue, green_cover, 1.0 - cover
            else:
                low = low + transmit * red_blue
                high = high + transmit * green_cover
                transmit = transmit * (1.0 - cover)
        low = low * jnp.where(low_rows, scales[0], scales[2])
        high = high * jnp.where(low_rows, scales[1], 1.0)
        image_ref[0, :, lanes_of(t)] = low[:4]
        image_ref[1, :, lanes_of(t)] = high[:4]
        image_ref[2, :, lanes_of(t)] = low[4:]
        coverage_ref[:, lanes_of(t)] = high[4:]


def neighbours(last, initial, axis):
    count = lax.axis_size(axis)
    up = [(i, i + 1) for i in range(count - 1)]
    down = [(j, i) for i, j in up]
    return lax.ppermute(last, axis, up), lax.ppermute(initial, axis, down)


def cost(flops, moved):
    return pl.CostEstimate(flops=flops, bytes_accessed=moved, transcendentals=0)


def on_device(volume, knot_bins, tf_colour, tf_density):
    depth, rows, cols = volume.shape
    count = lax.axis_size("gz")
    tiles = cols // LANES
    depth_total = float(depth * count)
    smem = pl.BlockSpec(memory_space=pltpu.SMEM)
    vmem = pl.BlockSpec(memory_space=pltpu.VMEM)
    params = pltpu.CompilerParams(vmem_limit_bytes=24 << 20)
    f32 = jnp.float32

    def whole(*shape):
        return pl.BlockSpec(shape, lambda n: (0,) * len(shape))

    top, bottom, y_edges, front, rear = pl.pallas_call(
        edges_kernel,
        grid=(1,),
        out_shape=(
            jax.ShapeDtypeStruct((depth, cols), volume.dtype),
            jax.ShapeDtypeStruct((depth, cols), volume.dtype),
            jax.ShapeDtypeStruct((rows, LANES), f32),
            jax.ShapeDtypeStruct((rows, cols), volume.dtype),
            jax.ShapeDtypeStruct((rows, cols), volume.dtype),
        ),
        in_specs=[
            pl.BlockSpec((depth, 16, cols), lambda n: (0, 0, 0)),
            pl.BlockSpec((depth, 16, cols), lambda n: (0, rows // 16 - 1, 0)),
            pl.BlockSpec((depth, rows, LANES), lambda n: (0, 0, 0)),
            pl.BlockSpec((depth, rows, LANES), lambda n: (0, 0, tiles - 1)),
            pl.BlockSpec((1, rows, cols), lambda n: (0, 0, 0)),
            pl.BlockSpec((1, rows, cols), lambda n: (depth - 1, 0, 0)),
        ],
        out_specs=(whole(depth, cols), whole(depth, cols), whole(rows, LANES), whole(rows, cols), whole(rows, cols)),
        scratch_shapes=[pltpu.VMEM((2, depth, cols), f32)],
        compiler_params=params,
        cost_estimate=cost(1 << 20, 2 << 20),
        name="edges",
    )(*[volume] * 6)
    bz, az = neighbours(rear, front, "gz")
    by, ay = neighbours(y_edges, y_edges, "gy")
    bx, ax = neighbours(bottom, top, "gx")
    spread_shape = jax.ShapeDtypeStruct((tiles, depth, rows + 2 * MARGIN, LANES), f32)
    consts_shape = jax.ShapeDtypeStruct((SCALES + 3, SUB, LANES), f32)
    cells, grads, consts = pl.pallas_call(
        functools.partial(spread_kernel, depth_total=depth_total),
        out_shape=(spread_shape, spread_shape, consts_shape),
        in_specs=[smem] * 3 + [vmem],
        out_specs=(vmem,) * 3,
        compiler_params=params,
        cost_estimate=cost(1 << 23, 2 << 20),
        name="spread",
    )(knot_bins, tf_colour, tf_density, volume)
    sent = jax.ShapeDtypeStruct((4, tiles, SUB, LANES), jnp.int32)
    work = cost(1 << 26, 1 << 22)
    arrived = {}

    def send(words, mate):
        arrived[mate] = lax.ppermute(words, "gz", [(i, i ^ mate) for i in range(count)])

    words, cells, grads, sides = pl.pallas_call(
        functools.partial(first_kernel, mate=2, depth_total=depth_total),
        out_shape=(
            sent,
            spread_shape,
            spread_shape,
            jax.ShapeDtypeStruct((2, tiles, rows + 2 * MARGIN, LANES), f32),
        ),
        in_specs=[vmem] * 9,
        out_specs=(vmem,) * 4,
        input_output_aliases={1: 1, 2: 2},
        compiler_params=params,
        cost_estimate=work,
        name="first",
    )(consts, cells, grads, bx, ax, by, ay, bz, az)
    send(words, 2)
    later_specs = [vmem] * 4 + [pl.BlockSpec(memory_space=pl.ANY)]
    for mate, behind in ((3, words), (1, arrived[2])):
        words = pl.pallas_call(
            functools.partial(later_kernel, mate=mate, depth_total=depth_total),
            out_shape=sent,
            in_specs=later_specs,
            out_specs=vmem,
            compiler_params=params,
            cost_estimate=work,
            name="later",
        )(consts, cells, grads, sides, behind)
        send(words, mate)
    ours = pl.pallas_call(
        functools.partial(ours_kernel, depth_total=depth_total),
        out_shape=jax.ShapeDtypeStruct((8, tiles, SUB, LANES), f32),
        in_specs=later_specs,
        out_specs=vmem,
        compiler_params=params,
        cost_estimate=work,
        name="ours",
    )(consts, cells, grads, sides, arrived[3])
    quads = count // QUAD
    codes = pl.pallas_call(
        quad_kernel,
        out_shape=jax.ShapeDtypeStruct((quads * tiles * SUB, LANES), jnp.int32),
        in_specs=[vmem] * 4,
        out_specs=vmem,
        compiler_params=params,
        name="quad",
    )(ours, arrived[1], arrived[2], arrived[3])
    pieces = lax.all_to_all(
        codes.reshape(quads, tiles * SUB, LANES),
        "gz",
        split_axis=0,
        concat_axis=0,
        tiled=True,
        axis_index_groups=[[QUAD * i + e for i in range(quads)] for e in range(QUAD)],
    )
    band = rows // count
    return pl.pallas_call(
        compose_kernel,
        out_shape=(
            jax.ShapeDtypeStruct((3, band, cols), f32),
            jax.ShapeDtypeStruct((band, cols), f32),
        ),
        in_specs=[vmem, vmem],
        out_specs=(vmem, vmem),
        name="compose",
    )(consts, pieces)


def solution(mesh):
    placed = (P("gz", "gx", "gy"), P(), P(), P())
    return jax.shard_map(
        on_device,
        mesh=mesh,
        in_specs=placed,
        out_specs=(P(None, ("gx", "gz"), "gy"), P(("gx", "gz"), "gy")),
        check_vma=False,
    )
```

```python
import functools
import math

import jax
import jax.numpy as jnp
import numpy as np
from jax import lax
from jax.experimental import pallas as pl
from jax.experimental.pallas import tpu as pltpu
from jax.sharding import PartitionSpec as P

BINS = 256
KNOTS = 8
SEGMENTS = KNOTS - 1
AMBIENT = 0.2
LANES = 128
SUB = 8
QUAD = 4
STEP = 4
MARGIN = 4
SCALES = 38

COLOUR_SPAN = 26.0
COVER_SPAN = 9.0
CODES = 65534.0


def colour_scale(colour_ref, channel):
    largest = colour_ref[channel, 0]
    for k in range(1, KNOTS):
        largest = jnp.maximum(largest, colour_ref[channel, k])
    return jnp.maximum(largest, 1e-30)


def encode(value, span):
    position = (jnp.log2(jnp.maximum(value, 2.0 ** (-span - 1.0))) + span) * (CODES / span) + 1.5
    return jnp.clip(position, 0.0, 65535.0).astype(jnp.int32)


def opacity_terms(largest):
    half = 0.5 * largest
    nodes = [half + half * math.cos(math.pi * (2 * i + 1) / 6.0) for i in range(3)]
    values = [-math.expm1(-y) / y for y in nodes]
    c0, c1, c2 = (float(c) for c in np.polynomial.polynomial.polyfit(nodes, values, 2))
    k = c2 ** (1.0 / 3.0)
    a = c1 / (2.0 * k * k)
    return k, a, c0 / k - a * a


def full(x):
    return jnp.full((SUB, LANES), x, jnp.float32)


def lanes_of(t):
    return slice(t * LANES, (t + 1) * LANES)


def lane_index():
    return lax.broadcasted_iota(jnp.int32, (SUB, LANES), 1)


def edges_kernel(x_low, x_high, y_low, y_high, z_low, z_high, top, bottom, y_out, front, rear, rows_x):
    depth = x_low.shape[0]
    cols = x_low.shape[2]
    for z in range(depth):
        low = x_low[z].astype(jnp.float32)
        high = x_high[z].astype(jnp.float32)
        rows_x[0, z:z + 1, :] = low[:1]
        rows_x[1, z:z + 1, :] = high[15:]
    top[...] = rows_x[0].astype(top.dtype)
    bottom[...] = rows_x[1].astype(bottom.dtype)
    lane = lane_index()
    for i in range(y_low.shape[1] // 16):
        sides = [jnp.zeros((SUB, LANES), jnp.float32)] * 2
        for z in range(depth):
            low = y_low[z, 16 * i:16 * i + 16, :].astype(jnp.float32)
            high = y_high[z, 16 * i:16 * i + 16, :].astype(jnp.float32)
            for part in range(2):
                at = slice(8 * part, 8 * part + 8)
                sides[part] = jnp.where(lane == z, low[at, :1], sides[part])
                sides[part] = jnp.where(lane == depth + z, high[at, LANES - 1:], sides[part])
        for part in range(2):
            y_out[pl.ds(SUB * STEP * part + i, SUB, stride=STEP), :] = sides[part]
    front[...] = z_low[0]
    rear[...] = z_high[0]


def slots_of(i):
    return pl.ds(MARGIN + SUB * STEP * (i % 2) + i // 2, SUB, stride=STEP)


def spread_kernel(knots_ref, colour_ref, density_ref, vol_ref, cells, grads, consts, *, depth_total):
    depth, rows, cols = vol_ref.shape
    lane = lax.broadcasted_iota(jnp.int32, (16, LANES), 1)
    tiles = cols // LANES
    prepare(consts, knots_ref, colour_ref, density_ref, depth_total)

    def step(z, carry):
        for c in range(rows // 16):
            plane = vol_ref[z, 16 * c:16 * c + 16, :].astype(jnp.float32)
            left = pltpu.roll(plane, 1, 1)
            right = pltpu.roll(plane, cols - 1, 1)
            for t in range(tiles):
                l, r = left[:, lanes_of(t)], right[:, lanes_of(t)]
                if t == 0:
                    l = jnp.where(lane == 0, 0.0, l)
                if t == tiles - 1:
                    r = jnp.where(lane == LANES - 1, 0.0, r)
                across = r - l
                own = plane[:, lanes_of(t)]
                for part in range(2):
                    at = slice(8 * part, 8 * part + 8)
                    cells[t, z, slots_of(2 * c + part), :] = own[at]
                    grads[t, z, slots_of(2 * c + part), :] = across[at]
                if c:
                    slot = MARGIN + rows + c - 1
                    cells[t, z, slot:slot + 1, :] = own[:1]
                if c < rows // 16 - 1:
                    cells[t, z, c + 1:c + 2, :] = own[15:]
        return carry

    lax.fori_loop(0, depth, step, 0)


def prepare(consts, knots_ref, colour_ref, density_ref, depth_total):
    top = BINS - 1.0
    spans = []
    for k in range(SEGMENTS):
        low = full(knots_ref[k].astype(jnp.float32))
        high = full(knots_ref[k + 1].astype(jnp.float32))
        spans.append((high - low) * (1.0 / top))
        if k:
            consts[k - 1] = low / top
    unit = opacity_terms(10.0 / depth_total)[0] / depth_total
    consts[6] = full(density_ref[0]) * unit
    for k in range(SEGMENTS):
        step = full(density_ref[k + 1]) - full(density_ref[k])
        consts[7 + k] = step * unit / spans[k]
    for c in range(3):
        scale = full(colour_scale(colour_ref, c))
        consts[SCALES + c] = scale
        consts[14 + 8 * c] = full(colour_ref[c, 0]) / scale
        for k in range(SEGMENTS):
            step = full(colour_ref[c, k + 1]) - full(colour_ref[c, k])
            consts[15 + 8 * c + k] = step / scale / spans[k]


def composite(consts, cell, grad_x, grad_y, depth, depth_total):
    _, shift, rest = opacity_terms(10.0 / depth_total)
    points = [consts[k] for k in range(6)]
    first = consts[6]
    slopes = [consts[7 + k] for k in range(SEGMENTS)]
    transmit = jnp.ones((SUB, LANES), jnp.float32)
    weight = None
    moments = None
    earlier, now = cell(-1), cell(0)
    for z in range(depth):
        later = cell(z + 1)
        gx, gy, gz = grad_x(z), grad_y(z), later - earlier
        across = gy + gz
        facing = jnp.abs(gx + (across + across))
        shading = AMBIENT + facing * (
            ((1.0 - AMBIENT) / 3.0) * lax.rsqrt(gx * gx + gy * gy + (gz * gz + 1.0))
        )
        capped = [jnp.minimum(now, p) for p in points] + [now]
        ramps = [capped[0]] + [capped[k + 1] - capped[k] for k in range(6)]
        y = first
        for k in range(SEGMENTS):
            y = y + ramps[k] * slopes[k]
        shifted = y + shift
        taken = transmit * (y * (shifted * shifted + rest))
        transmit = transmit - taken
        shaded = taken * shading
        if z == 0:
            weight = shaded
            moments = [shaded * r for r in ramps]
        else:
            weight = weight + shaded
            moments = [m + shaded * r for m, r in zip(moments, ramps)]
        earlier, now = now, later
    values = []
    for c in range(3):
        value = weight * consts[14 + 8 * c]
        for k in range(SEGMENTS):
            value = value + moments[k] * consts[15 + 8 * c + k]
        values.append(value)
    return values + [1.0 - transmit]


def spread_side(ref, sides, side):
    for c in range(ref.shape[0] // 16):
        plane = ref[16 * c:16 * c + 16, :].astype(jnp.float32)
        for t in range(sides.shape[1]):
            for part in range(2):
                sides[side, t, slots_of(2 * c + part), :] = plane[8 * part:8 * part + 8, lanes_of(t)]


def place_edges(cells, grads, bx_ref, ax_ref, by_ref, ay_ref):
    tiles, depth, slots = cells.shape[:3]
    for slot, ref in ((0, bx_ref), (slots - 1, ax_ref)):
        edge = ref[...].astype(jnp.float32)
        for z in range(depth):
            for t in range(tiles):
                cells[t, z, slot:slot + 1, :] = edge[z:z + 1, lanes_of(t)]
    lane = lane_index()

    def step(g, carry):
        rows = pl.ds(pl.multiple_of(SUB * g, SUB), SUB)
        at = pl.ds(SUB * g + MARGIN, SUB)
        before, after = by_ref[rows, :], ay_ref[rows, :]
        for z in range(depth):
            first = jnp.where(lane == 0, before[:, depth + z:depth + z + 1], 0.0)
            last = jnp.where(lane == LANES - 1, after[:, z:z + 1], 0.0)
            grads[0, z, at, :] = grads[0, z, at, :] - first
            grads[tiles - 1, z, at, :] = grads[tiles - 1, z, at, :] + last
        return carry

    lax.fori_loop(0, by_ref.shape[0] // SUB, step, 0)


def quarter_loop(consts, cells, grads, sides, owner, depth_total, store):
    tiles, depth = cells.shape[:2]

    def step(t, carry):
        for p in range(2):
            start = MARGIN + STEP * (4 * owner + 2 * p)
            at, above, below = (pl.ds(start + shift, SUB) for shift in (0, -STEP, STEP))

            def cell(z):
                if z < 0:
                    return sides[0, t, at, :]
                if z == depth:
                    return sides[1, t, at, :]
                return cells[t, z, at, :]

            values = composite(
                consts,
                cell,
                lambda z: cells[t, z, below, :] - cells[t, z, above, :],
                lambda z: grads[t, z, at, :],
                depth,
                depth_total,
            )
            store(t, p, values)
        return carry

    lax.fori_loop(0, tiles, step, 0)


def pack(values):
    codes = [encode(v, COLOUR_SPAN) for v in values[:3]] + [encode(values[3], COVER_SPAN)]
    return codes[0] | (codes[1] << 16), codes[2] | (codes[3] << 16)


def decode(code, span):
    value = jnp.exp2(code.astype(jnp.float32) * (span / CODES) - (span + span / CODES))
    return jnp.where(code > 0, value, 0.0)


def place_in_quad():
    return lax.rem(lax.axis_index("gz"), QUAD)


def send_quarter(consts, cells, grads, sides, out_ref, mate, depth_total):
    def store(t, p, values):
        first, second = pack(values)
        out_ref[p, t] = first
        out_ref[2 + p, t] = second

    quarter_loop(consts, cells, grads, sides, place_in_quad() ^ mate, depth_total, store)


def first_kernel(
    consts, cells_in, grads_in, bx_ref, ax_ref, by_ref, ay_ref, bz_ref, az_ref,
    out_ref, cells, grads, sides, *, mate, depth_total,
):
    spread_side(bz_ref, sides, 0)
    spread_side(az_ref, sides, 1)
    place_edges(cells, grads, bx_ref, ax_ref, by_ref, ay_ref)
    send_quarter(consts, cells, grads, sides, out_ref, mate, depth_total)


def later_kernel(consts, cells, grads, sides, _, out_ref, *, mate, depth_total):
    send_quarter(consts, cells, grads, sides, out_ref, mate, depth_total)


def ours_kernel(consts, cells, grads, sides, _, out_ref, *, depth_total):
    def store(t, p, values):
        for c in range(4):
            out_ref[2 * c + p, t] = values[c]

    quarter_loop(consts, cells, grads, sides, place_in_quad(), depth_total, store)


def quad_index():
    return lax.axis_index("gz") // QUAD


def quad_kernel(ours_ref, mate1_ref, mate2_ref, mate3_ref, *refs):
    outs, out_ref = refs[:QUAD], refs[QUAD]
    tiles = ours_ref.shape[1]
    mates = (ours_ref, mate1_ref, mate2_ref, mate3_ref)

    def piece(k, t, p):
        if k == 0:
            return [ours_ref[2 * c + p, t] for c in range(4)]
        first, second = mates[k][p, t], mates[k][2 + p, t]
        return [
            decode(first & 0xFFFF, COLOUR_SPAN),
            decode(lax.shift_right_logical(first, 16), COLOUR_SPAN),
            decode(second & 0xFFFF, COLOUR_SPAN),
            decode(lax.shift_right_logical(second, 16), COVER_SPAN),
        ]

    for place in range(QUAD):

        @pl.when(place_in_quad() == place)
        def _():
            def step(t, carry):
                for p in range(2):
                    total = piece(place, t, p)
                    for other in range(1, QUAD):
                        rear = piece(place ^ other, t, p)
                        keep = 1.0 - total[3]
                        total = [a + keep * b for a, b in zip(total, rear)]
                    for w, word in enumerate(pack(total)):
                        for q in range(2):
                            row = t * SUB + 4 * w + 2 * p + q
                            out_ref[pl.ds(row, 4, stride=tiles * SUB), :] = word[4 * q:4 * q + 4]
                return carry

            lax.fori_loop(0, tiles, step, 0)

    rows = tiles * SUB
    for k, ref in enumerate(outs):
        start = pl.multiple_of((quad_index() ^ k) * rows, SUB)
        ref[...] = out_ref[pl.ds(start, rows), :]


def compose_kernel(consts, *refs):
    swapped, (image_ref, coverage_ref, pieces_ref) = refs[:QUAD], refs[QUAD:]
    count = QUAD
    for k, ref in enumerate(swapped):
        pieces_ref[quad_index() ^ k] = ref[...]
    low_rows = lax.broadcasted_iota(jnp.int32, (SUB, LANES), 0) < 4
    scales = [consts[SCALES + c] for c in range(3)]
    step = COLOUR_SPAN / CODES
    steps_hi = jnp.where(low_rows, step, COVER_SPAN / CODES)
    start_hi = jnp.where(low_rows, -COLOUR_SPAN - step, -COVER_SPAN - COVER_SPAN / CODES)

    def level(code, steps, start):
        value = jnp.exp2(code.astype(jnp.float32) * steps + start)
        return jnp.where(code > 0, value, 0.0)

    for t in range(pieces_ref.shape[1] // SUB):
        low = high = None
        transmit = None
        for piece in range(count):
            word = pieces_ref[piece, t * SUB:(t + 1) * SUB, :]
            red_blue = level(word & 0xFFFF, step, -COLOUR_SPAN - step)
            green_cover = level(lax.shift_right_logical(word, 16), steps_hi, start_hi)
            cover = jnp.where(low_rows, pltpu.roll(green_cover, 4, 0), green_cover)
            if piece == 0:
                low, high, transmit = red_blue, green_cover, 1.0 - cover
            else:
                low = low + transmit * red_blue
                high = high + transmit * green_cover
                transmit = transmit * (1.0 - cover)
        low = low * jnp.where(low_rows, scales[0], scales[2])
        high = high * jnp.where(low_rows, scales[1], 1.0)
        image_ref[0, :, lanes_of(t)] = low[:4]
        image_ref[1, :, lanes_of(t)] = high[:4]
        image_ref[2, :, lanes_of(t)] = low[4:]
        coverage_ref[:, lanes_of(t)] = high[4:]


def neighbours(last, initial, axis):
    count = lax.axis_size(axis)
    up = [(i, i + 1) for i in range(count - 1)]
    down = [(j, i) for i, j in up]
    return lax.ppermute(last, axis, up), lax.ppermute(initial, axis, down)


def cost(flops, moved):
    return pl.CostEstimate(flops=flops, bytes_accessed=moved, transcendentals=0)


def on_device(volume, knot_bins, tf_colour, tf_density):
    depth, rows, cols = volume.shape
    count = lax.axis_size("gz")
    tiles = cols // LANES
    depth_total = float(depth * count)
    smem = pl.BlockSpec(memory_space=pltpu.SMEM)
    vmem = pl.BlockSpec(memory_space=pltpu.VMEM)
    params = pltpu.CompilerParams(vmem_limit_bytes=24 << 20)
    f32 = jnp.float32

    def whole(*shape):
        return pl.BlockSpec(shape, lambda n: (0,) * len(shape))

    top, bottom, y_edges, front, rear = pl.pallas_call(
        edges_kernel,
        grid=(1,),
        out_shape=(
            jax.ShapeDtypeStruct((depth, cols), volume.dtype),
            jax.ShapeDtypeStruct((depth, cols), volume.dtype),
            jax.ShapeDtypeStruct((rows, LANES), f32),
            jax.ShapeDtypeStruct((rows, cols), volume.dtype),
            jax.ShapeDtypeStruct((rows, cols), volume.dtype),
        ),
        in_specs=[
            pl.BlockSpec((depth, 16, cols), lambda n: (0, 0, 0)),
            pl.BlockSpec((depth, 16, cols), lambda n: (0, rows // 16 - 1, 0)),
            pl.BlockSpec((depth, rows, LANES), lambda n: (0, 0, 0)),
            pl.BlockSpec((depth, rows, LANES), lambda n: (0, 0, tiles - 1)),
            pl.BlockSpec((1, rows, cols), lambda n: (0, 0, 0)),
            pl.BlockSpec((1, rows, cols), lambda n: (depth - 1, 0, 0)),
        ],
        out_specs=(whole(depth, cols), whole(depth, cols), whole(rows, LANES), whole(rows, cols), whole(rows, cols)),
        scratch_shapes=[pltpu.VMEM((2, depth, cols), f32)],
        compiler_params=params,
        cost_estimate=cost(1 << 20, 2 << 20),
        name="edges",
    )(*[volume] * 6)
    bz, az = neighbours(rear, front, "gz")
    by, ay = neighbours(y_edges, y_edges, "gy")
    bx, ax = neighbours(bottom, top, "gx")
    spread_shape = jax.ShapeDtypeStruct((tiles, depth, rows + 2 * MARGIN, LANES), f32)
    consts_shape = jax.ShapeDtypeStruct((SCALES + 3, SUB, LANES), f32)
    cells, grads, consts = pl.pallas_call(
        functools.partial(spread_kernel, depth_total=depth_total),
        out_shape=(spread_shape, spread_shape, consts_shape),
        in_specs=[smem] * 3 + [vmem],
        out_specs=(vmem,) * 3,
        compiler_params=params,
        cost_estimate=cost(1 << 23, 2 << 20),
        name="spread",
    )(knot_bins, tf_colour, tf_density, volume)
    sent = jax.ShapeDtypeStruct((4, tiles, SUB, LANES), jnp.int32)
    work = cost(1 << 26, 1 << 22)
    arrived = {}

    def send(words, mate):
        arrived[mate] = lax.ppermute(words, "gz", [(i, i ^ mate) for i in range(count)])

    words, cells, grads, sides = pl.pallas_call(
        functools.partial(first_kernel, mate=2, depth_total=depth_total),
        out_shape=(
            sent,
            spread_shape,
            spread_shape,
            jax.ShapeDtypeStruct((2, tiles, rows + 2 * MARGIN, LANES), f32),
        ),
        in_specs=[vmem] * 9,
        out_specs=(vmem,) * 4,
        input_output_aliases={1: 1, 2: 2},
        compiler_params=params,
        cost_estimate=work,
        name="first",
    )(consts, cells, grads, bx, ax, by, ay, bz, az)
    send(words, 2)
    later_specs = [vmem] * 4 + [pl.BlockSpec(memory_space=pl.ANY)]
    for mate, behind in ((3, words), (1, arrived[2])):
        words = pl.pallas_call(
            functools.partial(later_kernel, mate=mate, depth_total=depth_total),
            out_shape=sent,
            in_specs=later_specs,
            out_specs=vmem,
            compiler_params=params,
            cost_estimate=work,
            name="later",
        )(consts, cells, grads, sides, behind)
        send(words, mate)
    ours = pl.pallas_call(
        functools.partial(ours_kernel, depth_total=depth_total),
        out_shape=jax.ShapeDtypeStruct((8, tiles, SUB, LANES), f32),
        in_specs=later_specs,
        out_specs=vmem,
        compiler_params=params,
        cost_estimate=work,
        name="ours",
    )(consts, cells, grads, sides, arrived[3])
    piece = jax.ShapeDtypeStruct((tiles * SUB, LANES), jnp.int32)
    pieces = pl.pallas_call(
        quad_kernel,
        out_shape=(piece,) * QUAD,
        in_specs=[vmem] * QUAD,
        out_specs=(vmem,) * QUAD,
        scratch_shapes=[pltpu.VMEM((QUAD * tiles * SUB, LANES), jnp.int32)],
        compiler_params=params,
        name="quad",
    )(ours, arrived[1], arrived[2], arrived[3])
    swapped = {0: pieces[0]}
    for k in (2, 1, 3):
        swapped[k] = lax.ppermute(pieces[k], "gz", [(i, i ^ (QUAD * k)) for i in range(count)])
    band = rows // count
    return pl.pallas_call(
        compose_kernel,
        out_shape=(
            jax.ShapeDtypeStruct((3, band, cols), f32),
            jax.ShapeDtypeStruct((band, cols), f32),
        ),
        in_specs=[vmem] * (1 + QUAD),
        out_specs=(vmem, vmem),
        scratch_shapes=[pltpu.VMEM((QUAD, tiles * SUB, LANES), jnp.int32)],
        name="compose",
    )(consts, *[swapped[k] for k in range(QUAD)])


def solution(mesh):
    placed = (P("gz", "gx", "gy"), P(), P(), P())
    return jax.shard_map(
        on_device,
        mesh=mesh,
        in_specs=placed,
        out_specs=(P(None, ("gx", "gz"), "gy"), P(("gx", "gz"), "gy")),
        check_vma=False,
    )
```

```python
import functools
import math

import jax
import jax.numpy as jnp
import numpy as np
from jax import lax
from jax.experimental import pallas as pl
from jax.experimental.pallas import tpu as pltpu
from jax.sharding import PartitionSpec as P

BINS = 256
KNOTS = 8
SEGMENTS = KNOTS - 1
AMBIENT = 0.2
LANES = 128
SUB = 8
GROUPS = 8
PITCH = 9
ABOVE = PITCH * (GROUPS - 1) - 1
BELOW = GROUPS
SCALES = 38

COLOUR_SPAN = 26.0
COVER_SPAN = 9.0
CODES = 65534.0


def colour_scale(colour_ref, channel):
    largest = colour_ref[channel, 0]
    for k in range(1, KNOTS):
        largest = jnp.maximum(largest, colour_ref[channel, k])
    return jnp.maximum(largest, 1e-30)


def encode(value, span):
    position = (jnp.log2(jnp.maximum(value, 2.0 ** (-span - 1.0))) + span) * (CODES / span) + 1.5
    return jnp.clip(position, 0.0, 65535.0).astype(jnp.int32)


def opacity_terms(largest):
    half = 0.5 * largest
    nodes = [half + half * math.cos(math.pi * (2 * i + 1) / 6.0) for i in range(3)]
    values = [-math.expm1(-y) / y for y in nodes]
    c0, c1, c2 = (float(c) for c in np.polynomial.polynomial.polyfit(nodes, values, 2))
    k = c2 ** (1.0 / 3.0)
    a = c1 / (2.0 * k * k)
    return k, a, c0 / k - a * a


def full(x):
    return jnp.full((SUB, LANES), x, jnp.float32)


def lanes_of(t):
    return slice(t * LANES, (t + 1) * LANES)


def lane_index():
    return lax.broadcasted_iota(jnp.int32, (SUB, LANES), 1)


def edges_kernel(x_low, x_high, y_low, y_high, z_low, z_high, top, bottom, y_out, front, rear, rows_x):
    depth = x_low.shape[0]
    cols = x_low.shape[2]
    for z in range(depth):
        low = x_low[z].astype(jnp.float32)
        high = x_high[z].astype(jnp.float32)
        rows_x[0, z:z + 1, :] = low[:1]
        rows_x[1, z:z + 1, :] = high[15:]
    top[...] = rows_x[0].astype(top.dtype)
    bottom[...] = rows_x[1].astype(bottom.dtype)
    lane = lane_index()
    for i in range(y_low.shape[1] // 16):
        sides = [jnp.zeros((SUB, LANES), jnp.float32)] * 2
        for z in range(depth):
            low = y_low[z, 16 * i:16 * i + 16, :].astype(jnp.float32)
            high = y_high[z, 16 * i:16 * i + 16, :].astype(jnp.float32)
            for part in range(2):
                at = slice(8 * part, 8 * part + 8)
                sides[part] = jnp.where(lane == z, low[at, :1], sides[part])
                sides[part] = jnp.where(lane == depth + z, high[at, LANES - 1:], sides[part])
        for part in range(2):
            y_out[pl.ds(2 * i + part, SUB, stride=GROUPS), :] = sides[part]
    front[...] = z_low[0]
    rear[...] = z_high[0]


def slots_of(i):
    return pl.ds(i, SUB, stride=PITCH)


def spread_kernel(knots_ref, colour_ref, density_ref, vol_ref, cells, grads, consts, *, depth_total):
    depth, rows, cols = vol_ref.shape
    lane = lax.broadcasted_iota(jnp.int32, (16, LANES), 1)
    tiles = cols // LANES
    prepare(consts, knots_ref, colour_ref, density_ref, depth_total)

    def step(z, carry):
        for c in range(rows // 16):
            plane = vol_ref[z, 16 * c:16 * c + 16, :].astype(jnp.float32)
            left = pltpu.roll(plane, 1, 1)
            right = pltpu.roll(plane, cols - 1, 1)
            for t in range(tiles):
                l, r = left[:, lanes_of(t)], right[:, lanes_of(t)]
                if t == 0:
                    l = jnp.where(lane == 0, 0.0, l)
                if t == tiles - 1:
                    r = jnp.where(lane == LANES - 1, 0.0, r)
                across = r - l
                own = plane[:, lanes_of(t)]
                for part in range(2):
                    at = slice(8 * part, 8 * part + 8)
                    cells[t, z, slots_of(2 * c + part), :] = own[at]
                    grads[t, z, slots_of(2 * c + part), :] = across[at]
        return carry

    lax.fori_loop(0, depth, step, 0)


def prepare(consts, knots_ref, colour_ref, density_ref, depth_total):
    top = BINS - 1.0
    spans = []
    for k in range(SEGMENTS):
        low = full(knots_ref[k].astype(jnp.float32))
        high = full(knots_ref[k + 1].astype(jnp.float32))
        spans.append((high - low) * (1.0 / top))
        if k:
            consts[k - 1] = low / top
    unit = opacity_terms(10.0 / depth_total)[0] / depth_total
    consts[6] = full(density_ref[0]) * unit
    for k in range(SEGMENTS):
        step = full(density_ref[k + 1]) - full(density_ref[k])
        consts[7 + k] = step * unit / spans[k]
    for c in range(3):
        scale = full(colour_scale(colour_ref, c))
        consts[SCALES + c] = scale
        consts[14 + 8 * c] = full(colour_ref[c, 0]) / scale
        for k in range(SEGMENTS):
            step = full(colour_ref[c, k + 1]) - full(colour_ref[c, k])
            consts[15 + 8 * c + k] = step / scale / spans[k]


def composite(consts, cell, grad_x, grad_y, depth, depth_total):
    _, shift, rest = opacity_terms(10.0 / depth_total)
    points = [consts[k] for k in range(6)]
    first = consts[6]
    slopes = [consts[7 + k] for k in range(SEGMENTS)]
    transmit = jnp.ones((SUB, LANES), jnp.float32)
    weight = None
    moments = None
    earlier, now = cell(-1), cell(0)
    for z in range(depth):
        later = cell(z + 1)
        gx, gy, gz = grad_x(z), grad_y(z), later - earlier
        across = gy + gz
        facing = jnp.abs(gx + (across + across))
        shading = AMBIENT + facing * (
            ((1.0 - AMBIENT) / 3.0) * lax.rsqrt(gx * gx + gy * gy + (gz * gz + 1.0))
        )
        capped = [jnp.minimum(now, p) for p in points] + [now]
        ramps = [capped[0]] + [capped[k + 1] - capped[k] for k in range(6)]
        y = first
        for k in range(SEGMENTS):
            y = y + ramps[k] * slopes[k]
        shifted = y + shift
        taken = transmit * (y * (shifted * shifted + rest))
        transmit = transmit - taken
        shaded = taken * shading
        if z == 0:
            weight = shaded
            moments = [shaded * r for r in ramps]
        else:
            weight = weight + shaded
            moments = [m + shaded * r for m, r in zip(moments, ramps)]
        earlier, now = now, later
    values = []
    for c in range(3):
        value = weight * consts[14 + 8 * c]
        for k in range(SEGMENTS):
            value = value + moments[k] * consts[15 + 8 * c + k]
        values.append(value)
    return values + [1.0 - transmit]


def spread_side(ref, sides, side):
    for c in range(ref.shape[0] // 16):
        plane = ref[16 * c:16 * c + 16, :].astype(jnp.float32)
        for t in range(sides.shape[1]):
            for part in range(2):
                sides[side, t, slots_of(2 * c + part), :] = plane[8 * part:8 * part + 8, lanes_of(t)]


def place_edges(cells, grads, bx_ref, ax_ref, by_ref, ay_ref, parity):
    tiles, depth = cells.shape[:2]
    slot = jnp.where(parity == 0, ABOVE, BELOW)
    edge = jnp.where(parity == 0, bx_ref[...].astype(jnp.float32), ax_ref[...].astype(jnp.float32))
    for z in range(depth):
        for t in range(tiles):
            cells[t, z, pl.ds(slot, 1), :] = edge[z:z + 1, lanes_of(t)]
    lane = lane_index()

    def step(j, carry):
        r = 4 * parity + j
        rows = pl.ds(pl.multiple_of(SUB * r, SUB), SUB)
        at = pl.ds(PITCH * r, SUB)
        before, after = by_ref[rows, :], ay_ref[rows, :]
        for z in range(depth):
            first = jnp.where(lane == 0, before[:, depth + z:depth + z + 1], 0.0)
            last = jnp.where(lane == LANES - 1, after[:, z:z + 1], 0.0)
            grads[0, z, at, :] = grads[0, z, at, :] - first
            grads[tiles - 1, z, at, :] = grads[tiles - 1, z, at, :] + last
        return carry

    lax.fori_loop(0, 4, step, 0)


def half_loop(consts, cells, grads, sides, parity, depth_total, store):
    tiles, depth = cells.shape[:2]

    def work(t, j):
        r = 4 * parity + j
        at = pl.ds(PITCH * r, SUB)
        above = pl.ds(jnp.where(r == 0, ABOVE, PITCH * r - PITCH), SUB)
        below = pl.ds(jnp.where(r == GROUPS - 1, 1, PITCH * r + PITCH), SUB)

        def cell(z):
            if z < 0:
                return sides[0, t, at, :]
            if z == depth:
                return sides[1, t, at, :]
            return cells[t, z, at, :]

        values = composite(
            consts,
            cell,
            lambda z: cells[t, z, below, :] - cells[t, z, above, :],
            lambda z: grads[t, z, at, :],
            depth,
            depth_total,
        )
        store(t, j, values)

    def step(n, carry):
        t, j = n // 2, 2 * (n % 2)
        work(t, j)
        work(t, j + 1)
        return carry

    lax.fori_loop(0, 2 * tiles, step, 0)


def pack(values):
    codes = [encode(v, COLOUR_SPAN) for v in values[:3]] + [encode(values[3], COVER_SPAN)]
    return codes[0] | (codes[1] << 16), codes[2] | (codes[3] << 16)


def decode(code, span):
    value = jnp.exp2(code.astype(jnp.float32) * (span / CODES) - (span + span / CODES))
    return jnp.where(code > 0, value, 0.0)


def my_parity():
    return lax.rem(lax.axis_index("gz"), 2)


def theirs_kernel(
    consts, cells_in, grads_in, bx_ref, ax_ref, by_ref, ay_ref, bz_ref, az_ref,
    out_ref, cells, grads, sides, *, depth_total,
):
    parity = 1 - my_parity()
    spread_side(bz_ref, sides, 0)
    spread_side(az_ref, sides, 1)
    place_edges(cells, grads, bx_ref, ax_ref, by_ref, ay_ref, parity)

    def store(t, j, values):
        first, second = pack(values)
        out_ref[j, t] = first
        out_ref[4 + j, t] = second

    half_loop(consts, cells, grads, sides, parity, depth_total, store)


def ours_kernel(
    consts, cells_in, grads_in, bx_ref, ax_ref, by_ref, ay_ref, sides,
    out_ref, cells, grads, *, depth_total,
):
    parity = my_parity()
    place_edges(cells, grads, bx_ref, ax_ref, by_ref, ay_ref, parity)

    def store(t, j, values):
        for c in range(4):
            out_ref[4 * c + j, t] = values[c]

    half_loop(consts, cells, grads, sides, parity, depth_total, store)


def pair_kernel(ours_ref, theirs_ref, out_ref):
    tiles = ours_ref.shape[1]
    front = lax.rem(lax.axis_index("gz"), 2) == 0

    def step(t, carry):
        for j in range(4):
            ours = [ours_ref[4 * c + j, t] for c in range(4)]
            first, second = theirs_ref[j, t], theirs_ref[4 + j, t]
            theirs = [
                decode(first & 0xFFFF, COLOUR_SPAN),
                decode(lax.shift_right_logical(first, 16), COLOUR_SPAN),
                decode(second & 0xFFFF, COLOUR_SPAN),
                decode(lax.shift_right_logical(second, 16), COVER_SPAN),
            ]
            keep_ours = jnp.where(front, 1.0, 1.0 - theirs[3])
            keep_theirs = jnp.where(front, 1.0 - ours[3], 1.0)
            words = pack([o * keep_ours + p * keep_theirs for o, p in zip(ours, theirs)])
            for w in range(2):
                out_ref[pl.ds(t * SUB + 4 * w + j, SUB, stride=tiles * SUB), :] = words[w]
        return carry

    lax.fori_loop(0, tiles, step, 0)


def compose_kernel(consts, pieces_ref, image_ref, coverage_ref):
    count = pieces_ref.shape[0]
    low_rows = lax.broadcasted_iota(jnp.int32, (SUB, LANES), 0) < 4
    scales = [consts[SCALES + c] for c in range(3)]
    step = COLOUR_SPAN / CODES
    steps_hi = jnp.where(low_rows, step, COVER_SPAN / CODES)
    start_hi = jnp.where(low_rows, -COLOUR_SPAN - step, -COVER_SPAN - COVER_SPAN / CODES)

    def level(code, steps, start):
        value = jnp.exp2(code.astype(jnp.float32) * steps + start)
        return jnp.where(code > 0, value, 0.0)

    for t in range(pieces_ref.shape[1] // SUB):
        low = high = None
        transmit = None
        for piece in range(count):
            word = pieces_ref[piece, t * SUB:(t + 1) * SUB, :]
            red_blue = level(word & 0xFFFF, step, -COLOUR_SPAN - step)
            green_cover = level(lax.shift_right_logical(word, 16), steps_hi, start_hi)
            cover = jnp.where(low_rows, pltpu.roll(green_cover, 4, 0), green_cover)
            if piece == 0:
                low, high, transmit = red_blue, green_cover, 1.0 - cover
            else:
                low = low + transmit * red_blue
                high = high + transmit * green_cover
                transmit = transmit * (1.0 - cover)
        low = low * jnp.where(low_rows, scales[0], scales[2])
        high = high * jnp.where(low_rows, scales[1], 1.0)
        image_ref[0, :, lanes_of(t)] = low[:4]
        image_ref[1, :, lanes_of(t)] = high[:4]
        image_ref[2, :, lanes_of(t)] = low[4:]
        coverage_ref[:, lanes_of(t)] = high[4:]


def neighbours(last, initial, axis):
    count = lax.axis_size(axis)
    up = [(i, i + 1) for i in range(count - 1)]
    down = [(j, i) for i, j in up]
    return lax.ppermute(last, axis, up), lax.ppermute(initial, axis, down)


def cost(flops, moved):
    return pl.CostEstimate(flops=flops, bytes_accessed=moved, transcendentals=0)


def on_device(volume, knot_bins, tf_colour, tf_density):
    depth, rows, cols = volume.shape
    count = lax.axis_size("gz")
    tiles = cols // LANES
    depth_total = float(depth * count)
    smem = pl.BlockSpec(memory_space=pltpu.SMEM)
    vmem = pl.BlockSpec(memory_space=pltpu.VMEM)
    params = pltpu.CompilerParams(vmem_limit_bytes=24 << 20)
    f32 = jnp.float32

    def whole(*shape):
        return pl.BlockSpec(shape, lambda n: (0,) * len(shape))

    top, bottom, y_edges, front, rear = pl.pallas_call(
        edges_kernel,
        grid=(1,),
        out_shape=(
            jax.ShapeDtypeStruct((depth, cols), volume.dtype),
            jax.ShapeDtypeStruct((depth, cols), volume.dtype),
            jax.ShapeDtypeStruct((rows, LANES), f32),
            jax.ShapeDtypeStruct((rows, cols), volume.dtype),
            jax.ShapeDtypeStruct((rows, cols), volume.dtype),
        ),
        in_specs=[
            pl.BlockSpec((depth, 16, cols), lambda n: (0, 0, 0)),
            pl.BlockSpec((depth, 16, cols), lambda n: (0, rows // 16 - 1, 0)),
            pl.BlockSpec((depth, rows, LANES), lambda n: (0, 0, 0)),
            pl.BlockSpec((depth, rows, LANES), lambda n: (0, 0, tiles - 1)),
            pl.BlockSpec((1, rows, cols), lambda n: (0, 0, 0)),
            pl.BlockSpec((1, rows, cols), lambda n: (depth - 1, 0, 0)),
        ],
        out_specs=(whole(depth, cols), whole(depth, cols), whole(rows, LANES), whole(rows, cols), whole(rows, cols)),
        scratch_shapes=[pltpu.VMEM((2, depth, cols), f32)],
        compiler_params=params,
        cost_estimate=cost(1 << 20, 2 << 20),
        name="edges",
    )(*[volume] * 6)
    bz, az = neighbours(rear, front, "gz")
    by, ay = neighbours(y_edges, y_edges, "gy")
    bx, ax = neighbours(bottom, top, "gx")
    spread_shape = jax.ShapeDtypeStruct((tiles, depth, PITCH * GROUPS, LANES), f32)
    consts_shape = jax.ShapeDtypeStruct((SCALES + 3, SUB, LANES), f32)
    cells, grads, consts = pl.pallas_call(
        functools.partial(spread_kernel, depth_total=depth_total),
        out_shape=(spread_shape, spread_shape, consts_shape),
        in_specs=[smem] * 3 + [vmem],
        out_specs=(vmem,) * 3,
        compiler_params=params,
        cost_estimate=cost(1 << 23, 2 << 20),
        name="spread",
    )(knot_bins, tf_colour, tf_density, volume)
    work = cost(1 << 26, 1 << 23)
    theirs, cells, grads, sides = pl.pallas_call(
        functools.partial(theirs_kernel, depth_total=depth_total),
        out_shape=(
            jax.ShapeDtypeStruct((8, tiles, SUB, LANES), jnp.int32),
            spread_shape,
            spread_shape,
            jax.ShapeDtypeStruct((2, tiles, PITCH * GROUPS, LANES), f32),
        ),
        in_specs=[vmem] * 9,
        out_specs=(vmem,) * 4,
        input_output_aliases={1: 1, 2: 2},
        compiler_params=params,
        cost_estimate=work,
        name="theirs",
    )(consts, cells, grads, bx, ax, by, ay, bz, az)
    arrived = lax.ppermute(theirs, "gz", [(i, i ^ 1) for i in range(count)])
    ours, _, _ = pl.pallas_call(
        functools.partial(ours_kernel, depth_total=depth_total),
        out_shape=(jax.ShapeDtypeStruct((16, tiles, SUB, LANES), f32), spread_shape, spread_shape),
        in_specs=[vmem] * 8,
        out_specs=(vmem,) * 3,
        input_output_aliases={1: 1, 2: 2},
        compiler_params=params,
        cost_estimate=work,
        name="ours",
    )(consts, cells, grads, bx, ax, by, ay, sides)
    half = count // 2
    codes = pl.pallas_call(
        pair_kernel,
        out_shape=jax.ShapeDtypeStruct((half * tiles * SUB, LANES), jnp.int32),
        in_specs=[vmem] * 2,
        out_specs=vmem,
        compiler_params=params,
        name="pair",
    )(ours, arrived)
    pieces = lax.all_to_all(
        codes.reshape(half, tiles * SUB, LANES),
        "gz",
        split_axis=0,
        concat_axis=0,
        tiled=True,
        axis_index_groups=[[2 * i + e for i in range(half)] for e in range(2)],
    )
    band = rows // count
    return pl.pallas_call(
        compose_kernel,
        out_shape=(
            jax.ShapeDtypeStruct((3, band, cols), f32),
            jax.ShapeDtypeStruct((band, cols), f32),
        ),
        in_specs=[vmem, vmem],
        out_specs=(vmem, vmem),
        name="compose",
    )(consts, pieces)


def solution(mesh):
    placed = (P("gz", "gx", "gy"), P(), P(), P())
    return jax.shard_map(
        on_device,
        mesh=mesh,
        in_specs=placed,
        out_specs=(P(None, ("gx", "gz"), "gy"), P(("gx", "gz"), "gy")),
        check_vma=False,
    )
```

```python
import functools
import math

import jax
import jax.numpy as jnp
import numpy as np
from jax import lax
from jax.experimental import pallas as pl
from jax.experimental.pallas import tpu as pltpu
from jax.sharding import PartitionSpec as P

BINS = 256
KNOTS = 8
SEGMENTS = KNOTS - 1
AMBIENT = 0.2
DIFFUSE = (1.0 - AMBIENT) / 3.0
LANES = 128
SUB = 8
GROUPS = 8
PITCH = 9
ABOVE = PITCH * (GROUPS - 1) - 1
BELOW = GROUPS
SCALES = 38

COLOUR_SPAN = 26.0
COVER_SPAN = 9.0
CODES = 65534.0


def colour_scale(colour_ref, channel):
    largest = colour_ref[channel, 0]
    for k in range(1, KNOTS):
        largest = jnp.maximum(largest, colour_ref[channel, k])
    return jnp.maximum(largest, 1e-30)


def encode(value, span):
    position = (jnp.log2(jnp.maximum(value, 2.0 ** (-span - 1.0))) + span) * (CODES / span) + 1.5
    return jnp.clip(position, 0.0, 65535.0).astype(jnp.int32)


def opacity_terms(largest):
    half = 0.5 * largest
    nodes = [half + half * math.cos(math.pi * (2 * i + 1) / 6.0) for i in range(3)]
    values = [-math.expm1(-y) / y for y in nodes]
    c0, c1, c2 = (float(c) for c in np.polynomial.polynomial.polyfit(nodes, values, 2))
    k = c2 ** (1.0 / 3.0)
    a = c1 / (2.0 * k * k)
    return k, a, c0 / k - a * a


def full(x):
    return jnp.full((SUB, LANES), x, jnp.float32)


def lanes_of(t):
    return slice(t * LANES, (t + 1) * LANES)


def lane_index():
    return lax.broadcasted_iota(jnp.int32, (SUB, LANES), 1)


def is_even(axis):
    return lax.rem(lax.axis_index(axis), 2) == 0


def edges_kernel(x_low, x_high, y_low, y_high, z_low, z_high, x_first, x_second, y_out, z_first, z_second, rows_x):
    depth = x_low.shape[0]
    even_x, even_z = is_even("gx"), is_even("gz")
    for z in range(depth):
        low = x_low[z].astype(jnp.float32)
        high = x_high[z].astype(jnp.float32)
        rows_x[0, z:z + 1, :] = low[:1]
        rows_x[1, z:z + 1, :] = high[15:]
    top, bottom = rows_x[0], rows_x[1]
    x_first[...] = jnp.where(even_x, bottom, top).astype(x_first.dtype)
    x_second[...] = jnp.where(even_x, top, bottom).astype(x_second.dtype)
    lane = lane_index()
    for i in range(y_low.shape[1] // 16):
        sides = [jnp.zeros((SUB, LANES), jnp.float32)] * 2
        for z in range(depth):
            low = y_low[z, 16 * i:16 * i + 16, :].astype(jnp.float32)
            high = y_high[z, 16 * i:16 * i + 16, :].astype(jnp.float32)
            for part in range(2):
                at = slice(8 * part, 8 * part + 8)
                sides[part] = jnp.where(lane == z, low[at, :1], sides[part])
                sides[part] = jnp.where(lane == depth + z, high[at, LANES - 1:], sides[part])
        for part in range(2):
            y_out[pl.ds(2 * i + part, SUB, stride=GROUPS), :] = sides[part]

    @pl.when(even_z)
    def _():
        z_first[...] = z_high[0]
        z_second[...] = z_low[0]

    @pl.when(jnp.logical_not(even_z))
    def _():
        z_first[...] = z_low[0]
        z_second[...] = z_high[0]


def slots_of(i):
    return pl.ds(i, SUB, stride=PITCH)


def spread_kernel(knots_ref, colour_ref, density_ref, vol_ref, cells, grads, consts, *, depth_total):
    depth, rows, cols = vol_ref.shape
    lane = lax.broadcasted_iota(jnp.int32, (16, LANES), 1)
    tiles = cols // LANES
    prepare(consts, knots_ref, colour_ref, density_ref, depth_total)

    def step(z, carry):
        for c in range(rows // 16):
            plane = vol_ref[z, 16 * c:16 * c + 16, :].astype(jnp.float32)
            left = pltpu.roll(plane, 1, 1)
            right = pltpu.roll(plane, cols - 1, 1)
            for t in range(tiles):
                l, r = left[:, lanes_of(t)], right[:, lanes_of(t)]
                if t == 0:
                    l = jnp.where(lane == 0, 0.0, l)
                if t == tiles - 1:
                    r = jnp.where(lane == LANES - 1, 0.0, r)
                across = r - l
                own = plane[:, lanes_of(t)]
                for part in range(2):
                    at = slice(8 * part, 8 * part + 8)
                    cells[t, z, slots_of(2 * c + part), :] = own[at]
                    grads[t, z, slots_of(2 * c + part), :] = across[at]
        return carry

    lax.fori_loop(0, depth, step, 0)


def prepare(consts, knots_ref, colour_ref, density_ref, depth_total):
    top = BINS - 1.0
    slants = []
    for k in range(SEGMENTS):
        low = full(knots_ref[k].astype(jnp.float32))
        high = full(knots_ref[k + 1].astype(jnp.float32))
        slants.append(top / (high - low))
        if k:
            consts[k - 1] = low * (1.0 / top)
    unit = opacity_terms(10.0 / depth_total)[0] / depth_total
    consts[6] = full(density_ref[0]) * unit
    for k in range(SEGMENTS):
        step = full(density_ref[k + 1]) - full(density_ref[k])
        consts[7 + k] = step * unit * slants[k]
    for c in range(3):
        scale = full(colour_scale(colour_ref, c))
        consts[SCALES + c] = scale
        unscale = DIFFUSE / scale
        consts[14 + 8 * c] = full(colour_ref[c, 0]) * unscale
        for k in range(SEGMENTS):
            step = full(colour_ref[c, k + 1]) - full(colour_ref[c, k])
            consts[15 + 8 * c + k] = step * unscale * slants[k]


def composite(consts, cell, grad_x, grad_y, depth, depth_total):
    _, shift, rest = opacity_terms(10.0 / depth_total)
    points = [consts[k] for k in range(6)]
    first = consts[6]
    slopes = [consts[7 + k] for k in range(SEGMENTS)]
    transmit = jnp.ones((SUB, LANES), jnp.float32)
    weight = None
    moments = None
    earlier, now = cell(-1), cell(0)
    for z in range(depth):
        later = cell(z + 1)
        gx, gy, gz = grad_x(z), grad_y(z), later - earlier
        across = gy + gz
        facing = jnp.abs(gx + (across + across))
        shading = AMBIENT / DIFFUSE + facing * lax.rsqrt(gx * gx + gy * gy + (gz * gz + 1.0))
        capped = [jnp.minimum(now, p) for p in points] + [now]
        ramps = [capped[0]] + [capped[k + 1] - capped[k] for k in range(6)]
        y = first
        for k in range(SEGMENTS):
            y = y + ramps[k] * slopes[k]
        shifted = y + shift
        taken = transmit * (y * (shifted * shifted + rest))
        transmit = transmit - taken
        shaded = taken * shading
        if z == 0:
            weight = shaded
            moments = [shaded * r for r in ramps]
        else:
            weight = weight + shaded
            moments = [m + shaded * r for m, r in zip(moments, ramps)]
        earlier, now = now, later
    values = []
    for c in range(3):
        value = weight * consts[14 + 8 * c]
        for k in range(SEGMENTS):
            value = value + moments[k] * consts[15 + 8 * c + k]
        values.append(value)
    return values + [1.0 - transmit]


def spread_side(ref, sides, side):
    for c in range(ref.shape[0] // 16):
        plane = ref[16 * c:16 * c + 16, :].astype(jnp.float32)
        for t in range(sides.shape[1]):
            for part in range(2):
                sides[side, t, slots_of(2 * c + part), :] = plane[8 * part:8 * part + 8, lanes_of(t)]


def place_edges(cells, grads, x_first, x_second, y_first, y_second, parity):
    tiles, depth = cells.shape[:2]
    slot = jnp.where(parity == 0, ABOVE, BELOW)
    even_x, even_y = is_even("gx"), is_even("gy")
    second = (parity == 0) == even_x
    edge = jnp.where(second, x_second[...].astype(jnp.float32), x_first[...].astype(jnp.float32))
    for z in range(depth):
        for t in range(tiles):
            cells[t, z, pl.ds(slot, 1), :] = edge[z:z + 1, lanes_of(t)]
    lane = lane_index()

    def step(j, carry):
        r = 4 * parity + j
        rows = pl.ds(pl.multiple_of(SUB * r, SUB), SUB)
        at = pl.ds(PITCH * r, SUB)
        before = jnp.where(even_y, y_second[rows, :], y_first[rows, :])
        after = jnp.where(even_y, y_first[rows, :], y_second[rows, :])
        for z in range(depth):
            first = jnp.where(lane == 0, before[:, depth + z:depth + z + 1], 0.0)
            last = jnp.where(lane == LANES - 1, after[:, z:z + 1], 0.0)
            grads[0, z, at, :] = grads[0, z, at, :] - first
            grads[tiles - 1, z, at, :] = grads[tiles - 1, z, at, :] + last
        return carry

    lax.fori_loop(0, 4, step, 0)


def half_loop(consts, cells, grads, sides, parity, depth_total, store):
    tiles, depth = cells.shape[:2]

    def work(t, j):
        r = 4 * parity + j
        at = pl.ds(PITCH * r, SUB)
        above = pl.ds(jnp.where(r == 0, ABOVE, PITCH * r - PITCH), SUB)
        below = pl.ds(jnp.where(r == GROUPS - 1, 1, PITCH * r + PITCH), SUB)

        def cell(z):
            if z < 0:
                return sides[0, t, at, :]
            if z == depth:
                return sides[1, t, at, :]
            return cells[t, z, at, :]

        values = composite(
            consts,
            cell,
            lambda z: cells[t, z, below, :] - cells[t, z, above, :],
            lambda z: grads[t, z, at, :],
            depth,
            depth_total,
        )
        store(t, j, values)

    def step(n, carry):
        t, j = n // 2, 2 * (n % 2)
        work(t, j)
        work(t, j + 1)
        return carry

    lax.fori_loop(0, 2 * tiles, step, 0)


def pack(values):
    codes = [encode(v, COLOUR_SPAN) for v in values[:3]] + [encode(values[3], COVER_SPAN)]
    return codes[0] | (codes[1] << 16), codes[2] | (codes[3] << 16)


def decode(code, span):
    value = jnp.exp2(code.astype(jnp.float32) * (span / CODES) - (span + span / CODES))
    return jnp.where(code > 0, value, 0.0)


def my_parity():
    return lax.rem(lax.axis_index("gz"), 2)


def theirs_kernel(
    consts, cells_in, grads_in, x_first, x_second, y_first, y_second, z_first, z_second,
    out_ref, cells, grads, sides, *, depth_total,
):
    parity = 1 - my_parity()
    before = jnp.where(is_even("gz"), 1, 0)
    spread_side(z_first, sides, before)
    spread_side(z_second, sides, 1 - before)
    place_edges(cells, grads, x_first, x_second, y_first, y_second, parity)

    def store(t, j, values):
        first, second = pack(values)
        out_ref[j, t] = first
        out_ref[4 + j, t] = second

    half_loop(consts, cells, grads, sides, parity, depth_total, store)


def ours_kernel(
    consts, cells_in, grads_in, x_first, x_second, y_first, y_second, sides,
    out_ref, cells, grads, *, depth_total,
):
    parity = my_parity()
    place_edges(cells, grads, x_first, x_second, y_first, y_second, parity)

    def store(t, j, values):
        for c in range(4):
            out_ref[4 * c + j, t] = values[c]

    half_loop(consts, cells, grads, sides, parity, depth_total, store)


def pair_kernel(ours_ref, theirs_ref, out_ref):
    tiles = ours_ref.shape[1]
    front = lax.rem(lax.axis_index("gz"), 2) == 0

    def step(t, carry):
        for j in range(4):
            ours = [ours_ref[4 * c + j, t] for c in range(4)]
            first, second = theirs_ref[j, t], theirs_ref[4 + j, t]
            theirs = [
                decode(first & 0xFFFF, COLOUR_SPAN),
                decode(lax.shift_right_logical(first, 16), COLOUR_SPAN),
                decode(second & 0xFFFF, COLOUR_SPAN),
                decode(lax.shift_right_logical(second, 16), COVER_SPAN),
            ]
            keep_ours = jnp.where(front, 1.0, 1.0 - theirs[3])
            keep_theirs = jnp.where(front, 1.0 - ours[3], 1.0)
            words = pack([o * keep_ours + p * keep_theirs for o, p in zip(ours, theirs)])
            for w in range(2):
                out_ref[pl.ds(t * SUB + 4 * w + j, SUB, stride=tiles * SUB), :] = words[w]
        return carry

    lax.fori_loop(0, tiles, step, 0)


def compose_kernel(consts, pieces_ref, image_ref, coverage_ref):
    count = pieces_ref.shape[0]
    low_rows = lax.broadcasted_iota(jnp.int32, (SUB, LANES), 0) < 4
    scales = [consts[SCALES + c] for c in range(3)]
    step = COLOUR_SPAN / CODES
    steps_hi = jnp.where(low_rows, step, COVER_SPAN / CODES)
    start_hi = jnp.where(low_rows, -COLOUR_SPAN - step, -COVER_SPAN - COVER_SPAN / CODES)

    def level(code, steps, start):
        value = jnp.exp2(code.astype(jnp.float32) * steps + start)
        return jnp.where(code > 0, value, 0.0)

    for t in range(pieces_ref.shape[1] // SUB):
        low = high = None
        transmit = None
        for piece in range(count):
            word = pieces_ref[piece, t * SUB:(t + 1) * SUB, :]
            red_blue = level(word & 0xFFFF, step, -COLOUR_SPAN - step)
            green_cover = level(lax.shift_right_logical(word, 16), steps_hi, start_hi)
            cover = jnp.where(low_rows, pltpu.roll(green_cover, 4, 0), green_cover)
            if piece == 0:
                low, high, transmit = red_blue, green_cover, 1.0 - cover
            else:
                low = low + transmit * red_blue
                high = high + transmit * green_cover
                transmit = transmit * (1.0 - cover)
        low = low * jnp.where(low_rows, scales[0], scales[2])
        high = high * jnp.where(low_rows, scales[1], 1.0)
        image_ref[0, :, lanes_of(t)] = low[:4]
        image_ref[1, :, lanes_of(t)] = high[:4]
        image_ref[2, :, lanes_of(t)] = low[4:]
        coverage_ref[:, lanes_of(t)] = high[4:]


def meet(first, second, axis):
    count = lax.axis_size(axis)

    def swap(edge, start):
        pairs = [(i, i + 1) for i in range(start, count - 1, 2)]
        return lax.ppermute(edge, axis, pairs + [(j, i) for i, j in pairs])

    return swap(first, 0), swap(second, 1)


def cost(flops, moved):
    return pl.CostEstimate(flops=flops, bytes_accessed=moved, transcendentals=0)


def on_device(volume, knot_bins, tf_colour, tf_density):
    depth, rows, cols = volume.shape
    count = lax.axis_size("gz")
    tiles = cols // LANES
    depth_total = float(depth * count)
    smem = pl.BlockSpec(memory_space=pltpu.SMEM)
    vmem = pl.BlockSpec(memory_space=pltpu.VMEM)
    params = pltpu.CompilerParams(vmem_limit_bytes=24 << 20)
    f32 = jnp.float32

    def whole(*shape):
        return pl.BlockSpec(shape, lambda n: (0,) * len(shape))

    x_first, x_second, y_edges, z_first, z_second = pl.pallas_call(
        edges_kernel,
        grid=(1,),
        out_shape=(
            jax.ShapeDtypeStruct((depth, cols), volume.dtype),
            jax.ShapeDtypeStruct((depth, cols), volume.dtype),
            jax.ShapeDtypeStruct((rows, LANES), f32),
            jax.ShapeDtypeStruct((rows, cols), volume.dtype),
            jax.ShapeDtypeStruct((rows, cols), volume.dtype),
        ),
        in_specs=[
            pl.BlockSpec((depth, 16, cols), lambda n: (0, 0, 0)),
            pl.BlockSpec((depth, 16, cols), lambda n: (0, rows // 16 - 1, 0)),
            pl.BlockSpec((depth, rows, LANES), lambda n: (0, 0, 0)),
            pl.BlockSpec((depth, rows, LANES), lambda n: (0, 0, tiles - 1)),
            pl.BlockSpec((1, rows, cols), lambda n: (0, 0, 0)),
            pl.BlockSpec((1, rows, cols), lambda n: (depth - 1, 0, 0)),
        ],
        out_specs=(whole(depth, cols), whole(depth, cols), whole(rows, LANES), whole(rows, cols), whole(rows, cols)),
        scratch_shapes=[pltpu.VMEM((2, depth, cols), f32)],
        compiler_params=params,
        cost_estimate=cost(1 << 20, 2 << 20),
        name="edges",
    )(*[volume] * 6)
    z_got = meet(z_first, z_second, "gz")
    y_got = meet(y_edges, y_edges, "gy")
    x_got = meet(x_first, x_second, "gx")
    spread_shape = jax.ShapeDtypeStruct((tiles, depth, PITCH * GROUPS, LANES), f32)
    consts_shape = jax.ShapeDtypeStruct((SCALES + 3, SUB, LANES), f32)
    cells, grads, consts = pl.pallas_call(
        functools.partial(spread_kernel, depth_total=depth_total),
        out_shape=(spread_shape, spread_shape, consts_shape),
        in_specs=[smem] * 3 + [vmem],
        out_specs=(vmem,) * 3,
        compiler_params=params,
        cost_estimate=cost(1 << 23, 2 << 20),
        name="spread",
    )(knot_bins, tf_colour, tf_density, volume)
    work = cost(1 << 26, 1 << 23)
    theirs, cells, grads, sides = pl.pallas_call(
        functools.partial(theirs_kernel, depth_total=depth_total),
        out_shape=(
            jax.ShapeDtypeStruct((8, tiles, SUB, LANES), jnp.int32),
            spread_shape,
            spread_shape,
            jax.ShapeDtypeStruct((2, tiles, PITCH * GROUPS, LANES), f32),
        ),
        in_specs=[vmem] * 9,
        out_specs=(vmem,) * 4,
        input_output_aliases={1: 1, 2: 2},
        compiler_params=params,
        cost_estimate=work,
        name="theirs",
    )(consts, cells, grads, *x_got, *y_got, *z_got)
    arrived = lax.ppermute(theirs, "gz", [(i, i ^ 1) for i in range(count)])
    ours, _, _ = pl.pallas_call(
        functools.partial(ours_kernel, depth_total=depth_total),
        out_shape=(jax.ShapeDtypeStruct((16, tiles, SUB, LANES), f32), spread_shape, spread_shape),
        in_specs=[vmem] * 8,
        out_specs=(vmem,) * 3,
        input_output_aliases={1: 1, 2: 2},
        compiler_params=params,
        cost_estimate=work,
        name="ours",
    )(consts, cells, grads, *x_got, *y_got, sides)
    half = count // 2
    codes = pl.pallas_call(
        pair_kernel,
        out_shape=jax.ShapeDtypeStruct((half * tiles * SUB, LANES), jnp.int32),
        in_specs=[vmem] * 2,
        out_specs=vmem,
        compiler_params=params,
        name="pair",
    )(ours, arrived)
    pieces = lax.all_to_all(
        codes.reshape(half, tiles * SUB, LANES),
        "gz",
        split_axis=0,
        concat_axis=0,
        tiled=True,
        axis_index_groups=[[2 * i + e for i in range(half)] for e in range(2)],
    )
    band = rows // count
    return pl.pallas_call(
        compose_kernel,
        out_shape=(
            jax.ShapeDtypeStruct((3, band, cols), f32),
            jax.ShapeDtypeStruct((band, cols), f32),
        ),
        in_specs=[vmem, vmem],
        out_specs=(vmem, vmem),
        name="compose",
    )(consts, pieces)


def solution(mesh):
    placed = (P("gz", "gx", "gy"), P(), P(), P())
    return jax.shard_map(
        on_device,
        mesh=mesh,
        in_specs=placed,
        out_specs=(P(None, ("gx", "gz"), "gy"), P(("gx", "gz"), "gy")),
        check_vma=False,
    )
```

```python
import functools
import math

import jax
import jax.numpy as jnp
import numpy as np
from jax import lax
from jax.experimental import pallas as pl
from jax.experimental.pallas import tpu as pltpu
from jax.sharding import PartitionSpec as P

BINS = 256
KNOTS = 8
SEGMENTS = KNOTS - 1
AMBIENT = 0.2
DIFFUSE = (1.0 - AMBIENT) / 3.0
LANES = 128
SUB = 8
GROUPS = 8
PITCH = 9
ABOVE = PITCH * (GROUPS - 1) - 1
BELOW = GROUPS
SCALES = 38

COLOUR_SPAN = 26.0
COVER_SPAN = 9.0
CODES = 65534.0


def colour_scale(colour_ref, channel):
    largest = colour_ref[channel, 0]
    for k in range(1, KNOTS):
        largest = jnp.maximum(largest, colour_ref[channel, k])
    return jnp.maximum(largest, 1e-30)


def encode(value, span):
    position = (jnp.log2(jnp.maximum(value, 2.0 ** (-span - 1.0))) + span) * (CODES / span) + 1.5
    return jnp.clip(position, 0.0, 65535.0).astype(jnp.int32)


def opacity_terms(largest):
    half = 0.5 * largest
    nodes = [half + half * math.cos(math.pi * (2 * i + 1) / 6.0) for i in range(3)]
    values = [-math.expm1(-y) / y for y in nodes]
    c0, c1, c2 = (float(c) for c in np.polynomial.polynomial.polyfit(nodes, values, 2))
    k = c2 ** (1.0 / 3.0)
    a = c1 / (2.0 * k * k)
    return k, a, c0 / k - a * a


def full(x):
    return jnp.full((SUB, LANES), x, jnp.float32)


def lanes_of(t):
    return slice(t * LANES, (t + 1) * LANES)


def lane_index():
    return lax.broadcasted_iota(jnp.int32, (SUB, LANES), 1)


def is_even(axis):
    return lax.rem(lax.axis_index(axis), 2) == 0


def edges_kernel(x_low, x_high, y_low, y_high, z_low, z_high, x_first, x_second, y_out, z_first, z_second, rows_x):
    depth = x_low.shape[0]
    even_x, even_z = is_even("gx"), is_even("gz")
    for z in range(depth):
        low = x_low[z].astype(jnp.float32)
        high = x_high[z].astype(jnp.float32)
        rows_x[0, z:z + 1, :] = low[:1]
        rows_x[1, z:z + 1, :] = high[15:]
    top, bottom = rows_x[0], rows_x[1]
    x_first[...] = jnp.where(even_x, bottom, top).astype(x_first.dtype)
    x_second[...] = jnp.where(even_x, top, bottom).astype(x_second.dtype)
    lane = lane_index()
    for i in range(y_low.shape[1] // 16):
        sides = [jnp.zeros((SUB, LANES), jnp.float32)] * 2
        for z in range(depth):
            low = y_low[z, 16 * i:16 * i + 16, :].astype(jnp.float32)
            high = y_high[z, 16 * i:16 * i + 16, :].astype(jnp.float32)
            for part in range(2):
                at = slice(8 * part, 8 * part + 8)
                sides[part] = jnp.where(lane == z, low[at, :1], sides[part])
                sides[part] = jnp.where(lane == depth + z, high[at, LANES - 1:], sides[part])
        for part in range(2):
            y_out[pl.ds(2 * i + part, SUB, stride=GROUPS), :] = sides[part]

    @pl.when(even_z)
    def _():
        z_first[...] = z_high[0]
        z_second[...] = z_low[0]

    @pl.when(jnp.logical_not(even_z))
    def _():
        z_first[...] = z_low[0]
        z_second[...] = z_high[0]


def slots_of(i):
    return pl.ds(i, SUB, stride=PITCH)


def spread_kernel(knots_ref, colour_ref, density_ref, vol_ref, cells, grads, consts, *, depth_total):
    depth, rows, cols = vol_ref.shape
    lane = lax.broadcasted_iota(jnp.int32, (16, LANES), 1)
    tiles = cols // LANES
    prepare(consts, knots_ref, colour_ref, density_ref, depth_total)

    def step(z, carry):
        for c in range(rows // 16):
            plane = vol_ref[z, 16 * c:16 * c + 16, :].astype(jnp.float32)
            left = pltpu.roll(plane, 1, 1)
            right = pltpu.roll(plane, cols - 1, 1)
            for t in range(tiles):
                l, r = left[:, lanes_of(t)], right[:, lanes_of(t)]
                if t == 0:
                    l = jnp.where(lane == 0, 0.0, l)
                if t == tiles - 1:
                    r = jnp.where(lane == LANES - 1, 0.0, r)
                across = r - l
                own = plane[:, lanes_of(t)]
                for part in range(2):
                    at = slice(8 * part, 8 * part + 8)
                    cells[t, z, slots_of(2 * c + part), :] = own[at]
                    grads[t, z, slots_of(2 * c + part), :] = across[at]
        return carry

    lax.fori_loop(0, depth, step, 0)


def prepare(consts, knots_ref, colour_ref, density_ref, depth_total):
    top = BINS - 1.0
    slants = []
    for k in range(SEGMENTS):
        low = full(knots_ref[k].astype(jnp.float32))
        high = full(knots_ref[k + 1].astype(jnp.float32))
        slants.append(top / (high - low))
        if k:
            consts[k - 1] = low * (1.0 / top)
    unit = opacity_terms(10.0 / depth_total)[0] / depth_total
    consts[6] = full(density_ref[0]) * unit
    for k in range(SEGMENTS):
        step = full(density_ref[k + 1]) - full(density_ref[k])
        consts[7 + k] = step * unit * slants[k]
    for c in range(3):
        scale = full(colour_scale(colour_ref, c))
        consts[SCALES + c] = scale
        unscale = DIFFUSE / scale
        consts[14 + 8 * c] = full(colour_ref[c, 0]) * unscale
        for k in range(SEGMENTS):
            step = full(colour_ref[c, k + 1]) - full(colour_ref[c, k])
            consts[15 + 8 * c + k] = step * unscale * slants[k]


def composite(consts, cell, grad_x, grad_y, depth, depth_total):
    _, shift, rest = opacity_terms(10.0 / depth_total)
    points = [consts[k] for k in range(6)]
    first = consts[6]
    slopes = [consts[7 + k] for k in range(SEGMENTS)]
    transmit = jnp.ones((SUB, LANES), jnp.float32)
    weight = None
    moments = None
    earlier, now = cell(-1), cell(0)
    for z in range(depth):
        later = cell(z + 1)
        gx, gy, gz = grad_x(z), grad_y(z), later - earlier
        across = gy + gz
        facing = jnp.abs(gx + (across + across))
        shading = AMBIENT / DIFFUSE + facing * lax.rsqrt(gx * gx + gy * gy + (gz * gz + 1.0))
        capped = [jnp.minimum(now, p) for p in points] + [now]
        ramps = [capped[0]] + [capped[k + 1] - capped[k] for k in range(6)]
        y = first
        for k in range(SEGMENTS):
            y = y + ramps[k] * slopes[k]
        shifted = y + shift
        taken = transmit * (y * (shifted * shifted + rest))
        transmit = transmit - taken
        shaded = taken * shading
        if z == 0:
            weight = shaded
            moments = [shaded * r for r in ramps]
        else:
            weight = weight + shaded
            moments = [m + shaded * r for m, r in zip(moments, ramps)]
        earlier, now = now, later
    values = []
    for c in range(3):
        value = weight * consts[14 + 8 * c]
        for k in range(SEGMENTS):
            value = value + moments[k] * consts[15 + 8 * c + k]
        values.append(value)
    return values + [1.0 - transmit]


def spread_side(ref, sides, side):
    for c in range(ref.shape[0] // 16):
        plane = ref[16 * c:16 * c + 16, :].astype(jnp.float32)
        for t in range(sides.shape[1]):
            for part in range(2):
                sides[side, t, slots_of(2 * c + part), :] = plane[8 * part:8 * part + 8, lanes_of(t)]


def place_edges(cells, grads, x_first, x_second, y_first, y_second, parity):
    tiles, depth = cells.shape[:2]
    slot = jnp.where(parity == 0, ABOVE, BELOW)
    even_x, even_y = is_even("gx"), is_even("gy")
    second = (parity == 0) == even_x
    edge = jnp.where(second, x_second[...].astype(jnp.float32), x_first[...].astype(jnp.float32))
    for z in range(depth):
        for t in range(tiles):
            cells[t, z, pl.ds(slot, 1), :] = edge[z:z + 1, lanes_of(t)]
    lane = lane_index()

    def step(j, carry):
        r = 4 * parity + j
        rows = pl.ds(pl.multiple_of(SUB * r, SUB), SUB)
        at = pl.ds(PITCH * r, SUB)
        before = jnp.where(even_y, y_second[rows, :], y_first[rows, :])
        after = jnp.where(even_y, y_first[rows, :], y_second[rows, :])
        for z in range(depth):
            first = jnp.where(lane == 0, before[:, depth + z:depth + z + 1], 0.0)
            last = jnp.where(lane == LANES - 1, after[:, z:z + 1], 0.0)
            grads[0, z, at, :] = grads[0, z, at, :] - first
            grads[tiles - 1, z, at, :] = grads[tiles - 1, z, at, :] + last
        return carry

    lax.fori_loop(0, 4, step, 0)


def half_loop(consts, cells, grads, sides, parity, depth_total, store):
    tiles, depth = cells.shape[:2]

    def work(t, j):
        r = 4 * parity + j
        at = pl.ds(PITCH * r, SUB)
        above = pl.ds(jnp.where(r == 0, ABOVE, PITCH * r - PITCH), SUB)
        below = pl.ds(jnp.where(r == GROUPS - 1, 1, PITCH * r + PITCH), SUB)

        def cell(z):
            if z < 0:
                return sides[0, t, at, :]
            if z == depth:
                return sides[1, t, at, :]
            return cells[t, z, at, :]

        values = composite(
            consts,
            cell,
            lambda z: cells[t, z, below, :] - cells[t, z, above, :],
            lambda z: grads[t, z, at, :],
            depth,
            depth_total,
        )
        store(t, j, values)

    def step(n, carry):
        t, j = n // 2, 2 * (n % 2)
        work(t, j)
        work(t, j + 1)
        return carry

    lax.fori_loop(0, 2 * tiles, step, 0)


def pack(values):
    codes = [encode(v, COLOUR_SPAN) for v in values[:3]] + [encode(values[3], COVER_SPAN)]
    return codes[0] | (codes[1] << 16), codes[2] | (codes[3] << 16)


def decode(code, span):
    value = jnp.exp2(code.astype(jnp.float32) * (span / CODES) - (span + span / CODES))
    return jnp.where(code > 0, value, 0.0)


def my_parity():
    return lax.rem(lax.axis_index("gz"), 2)


def theirs_kernel(
    consts, cells_in, grads_in, y_second, y_first, x_first, x_second, z_first, z_second,
    out_ref, cells, grads, sides, *, depth_total,
):
    parity = 1 - my_parity()
    before = jnp.where(is_even("gz"), 1, 0)
    spread_side(z_first, sides, before)
    spread_side(z_second, sides, 1 - before)
    place_edges(cells, grads, x_first, x_second, y_first, y_second, parity)

    def store(t, j, values):
        first, second = pack(values)
        out_ref[j, t] = first
        out_ref[4 + j, t] = second

    half_loop(consts, cells, grads, sides, parity, depth_total, store)


def ours_kernel(
    consts, cells_in, grads_in, y_second, y_first, x_first, x_second, sides,
    out_ref, cells, grads, *, depth_total,
):
    parity = my_parity()
    place_edges(cells, grads, x_first, x_second, y_first, y_second, parity)

    def store(t, j, values):
        for c in range(4):
            out_ref[4 * c + j, t] = values[c]

    half_loop(consts, cells, grads, sides, parity, depth_total, store)


def pair_kernel(ours_ref, theirs_ref, out_ref):
    tiles = ours_ref.shape[1]
    front = lax.rem(lax.axis_index("gz"), 2) == 0

    def step(t, carry):
        for j in range(4):
            ours = [ours_ref[4 * c + j, t] for c in range(4)]
            first, second = theirs_ref[j, t], theirs_ref[4 + j, t]
            theirs = [
                decode(first & 0xFFFF, COLOUR_SPAN),
                decode(lax.shift_right_logical(first, 16), COLOUR_SPAN),
                decode(second & 0xFFFF, COLOUR_SPAN),
                decode(lax.shift_right_logical(second, 16), COVER_SPAN),
            ]
            keep_ours = jnp.where(front, 1.0, 1.0 - theirs[3])
            keep_theirs = jnp.where(front, 1.0 - ours[3], 1.0)
            words = pack([o * keep_ours + p * keep_theirs for o, p in zip(ours, theirs)])
            for w in range(2):
                out_ref[pl.ds(t * SUB + 4 * w + j, SUB, stride=tiles * SUB), :] = words[w]
        return carry

    lax.fori_loop(0, tiles, step, 0)


def compose_kernel(consts, pieces_ref, image_ref, coverage_ref):
    count = pieces_ref.shape[0]
    low_rows = lax.broadcasted_iota(jnp.int32, (SUB, LANES), 0) < 4
    scales = [consts[SCALES + c] for c in range(3)]
    step = COLOUR_SPAN / CODES
    steps_hi = jnp.where(low_rows, step, COVER_SPAN / CODES)
    start_hi = jnp.where(low_rows, -COLOUR_SPAN - step, -COVER_SPAN - COVER_SPAN / CODES)

    def level(code, steps, start):
        value = jnp.exp2(code.astype(jnp.float32) * steps + start)
        return jnp.where(code > 0, value, 0.0)

    for t in range(pieces_ref.shape[1] // SUB):
        low = high = None
        transmit = None
        for piece in range(count):
            word = pieces_ref[piece, t * SUB:(t + 1) * SUB, :]
            red_blue = level(word & 0xFFFF, step, -COLOUR_SPAN - step)
            green_cover = level(lax.shift_right_logical(word, 16), steps_hi, start_hi)
            cover = jnp.where(low_rows, pltpu.roll(green_cover, 4, 0), green_cover)
            if piece == 0:
                low, high, transmit = red_blue, green_cover, 1.0 - cover
            else:
                low = low + transmit * red_blue
                high = high + transmit * green_cover
                transmit = transmit * (1.0 - cover)
        low = low * jnp.where(low_rows, scales[0], scales[2])
        high = high * jnp.where(low_rows, scales[1], 1.0)
        image_ref[0, :, lanes_of(t)] = low[:4]
        image_ref[1, :, lanes_of(t)] = high[:4]
        image_ref[2, :, lanes_of(t)] = low[4:]
        coverage_ref[:, lanes_of(t)] = high[4:]


def meet(first, second, axis):
    count = lax.axis_size(axis)

    def swap(edge, start):
        pairs = [(i, i + 1) for i in range(start, count - 1, 2)]
        return lax.ppermute(edge, axis, pairs + [(j, i) for i, j in pairs])

    return swap(first, 0), swap(second, 1)


def cost(flops, moved):
    return pl.CostEstimate(flops=flops, bytes_accessed=moved, transcendentals=0)


def on_device(volume, knot_bins, tf_colour, tf_density):
    depth, rows, cols = volume.shape
    count = lax.axis_size("gz")
    tiles = cols // LANES
    depth_total = float(depth * count)
    smem = pl.BlockSpec(memory_space=pltpu.SMEM)
    vmem = pl.BlockSpec(memory_space=pltpu.VMEM)
    params = pltpu.CompilerParams(vmem_limit_bytes=24 << 20)
    f32 = jnp.float32

    def whole(*shape):
        return pl.BlockSpec(shape, lambda n: (0,) * len(shape))

    x_first, x_second, y_edges, z_first, z_second = pl.pallas_call(
        edges_kernel,
        grid=(1,),
        out_shape=(
            jax.ShapeDtypeStruct((depth, cols), volume.dtype),
            jax.ShapeDtypeStruct((depth, cols), volume.dtype),
            jax.ShapeDtypeStruct((rows, LANES), f32),
            jax.ShapeDtypeStruct((rows, cols), volume.dtype),
            jax.ShapeDtypeStruct((rows, cols), volume.dtype),
        ),
        in_specs=[
            pl.BlockSpec((depth, 16, cols), lambda n: (0, 0, 0)),
            pl.BlockSpec((depth, 16, cols), lambda n: (0, rows // 16 - 1, 0)),
            pl.BlockSpec((depth, rows, LANES), lambda n: (0, 0, 0)),
            pl.BlockSpec((depth, rows, LANES), lambda n: (0, 0, tiles - 1)),
            pl.BlockSpec((1, rows, cols), lambda n: (0, 0, 0)),
            pl.BlockSpec((1, rows, cols), lambda n: (depth - 1, 0, 0)),
        ],
        out_specs=(whole(depth, cols), whole(depth, cols), whole(rows, LANES), whole(rows, cols), whole(rows, cols)),
        scratch_shapes=[pltpu.VMEM((2, depth, cols), f32)],
        compiler_params=params,
        cost_estimate=cost(1 << 20, 2 << 20),
        name="edges",
    )(*[volume] * 6)
    z_got = meet(z_first, z_second, "gz")
    y_got = meet(y_edges, y_edges, "gy")
    x_got = meet(x_first, x_second, "gx")
    spread_shape = jax.ShapeDtypeStruct((tiles, depth, PITCH * GROUPS, LANES), f32)
    consts_shape = jax.ShapeDtypeStruct((SCALES + 3, SUB, LANES), f32)
    cells, grads, consts = pl.pallas_call(
        functools.partial(spread_kernel, depth_total=depth_total),
        out_shape=(spread_shape, spread_shape, consts_shape),
        in_specs=[smem] * 3 + [vmem],
        out_specs=(vmem,) * 3,
        compiler_params=params,
        cost_estimate=cost(1 << 23, 2 << 20),
        name="spread",
    )(knot_bins, tf_colour, tf_density, volume)
    work = cost(1 << 26, 1 << 23)
    theirs, cells, grads, sides = pl.pallas_call(
        functools.partial(theirs_kernel, depth_total=depth_total),
        out_shape=(
            jax.ShapeDtypeStruct((8, tiles, SUB, LANES), jnp.int32),
            spread_shape,
            spread_shape,
            jax.ShapeDtypeStruct((2, tiles, PITCH * GROUPS, LANES), f32),
        ),
        in_specs=[vmem] * 9,
        out_specs=(vmem,) * 4,
        input_output_aliases={1: 1, 2: 2},
        compiler_params=params,
        cost_estimate=work,
        name="theirs",
    )(consts, cells, grads, *y_got[::-1], *x_got, *z_got)
    arrived = lax.ppermute(theirs, "gz", [(i, i ^ 1) for i in range(count)])
    ours, _, _ = pl.pallas_call(
        functools.partial(ours_kernel, depth_total=depth_total),
        out_shape=(jax.ShapeDtypeStruct((16, tiles, SUB, LANES), f32), spread_shape, spread_shape),
        in_specs=[vmem] * 8,
        out_specs=(vmem,) * 3,
        input_output_aliases={1: 1, 2: 2},
        compiler_params=params,
        cost_estimate=work,
        name="ours",
    )(consts, cells, grads, *y_got[::-1], *x_got, sides)
    half = count // 2
    codes = pl.pallas_call(
        pair_kernel,
        out_shape=jax.ShapeDtypeStruct((half * tiles * SUB, LANES), jnp.int32),
        in_specs=[vmem] * 2,
        out_specs=vmem,
        compiler_params=params,
        name="pair",
    )(ours, arrived)
    pieces = lax.all_to_all(
        codes.reshape(half, tiles * SUB, LANES),
        "gz",
        split_axis=0,
        concat_axis=0,
        tiled=True,
        axis_index_groups=[[2 * i + e for i in range(half)] for e in range(2)],
    )
    band = rows // count
    return pl.pallas_call(
        compose_kernel,
        out_shape=(
            jax.ShapeDtypeStruct((3, band, cols), f32),
            jax.ShapeDtypeStruct((band, cols), f32),
        ),
        in_specs=[vmem, vmem],
        out_specs=(vmem, vmem),
        name="compose",
    )(consts, pieces)


def solution(mesh):
    placed = (P("gz", "gx", "gy"), P(), P(), P())
    return jax.shard_map(
        on_device,
        mesh=mesh,
        in_specs=placed,
        out_specs=(P(None, ("gx", "gz"), "gy"), P(("gx", "gz"), "gy")),
        check_vma=False,
    )
```

```python
import functools
import math

import jax
import jax.numpy as jnp
import numpy as np
from jax import lax
from jax.experimental import pallas as pl
from jax.experimental.pallas import tpu as pltpu
from jax.sharding import PartitionSpec as P

BINS = 256
KNOTS = 8
SEGMENTS = KNOTS - 1
AMBIENT = 0.2
DIFFUSE = (1.0 - AMBIENT) / 3.0
LANES = 128
SUB = 8
GROUPS = 8
PITCH = 9
ABOVE = PITCH * (GROUPS - 1) - 1
BELOW = GROUPS
SCALES = 38

COLOUR_SPAN = 26.0
COVER_SPAN = 9.0
CODES = 65534.0


def colour_scale(colour_ref, channel):
    largest = colour_ref[channel, 0]
    for k in range(1, KNOTS):
        largest = jnp.maximum(largest, colour_ref[channel, k])
    return jnp.maximum(largest, 1e-30)


def encode(value, span):
    position = (jnp.log2(jnp.maximum(value, 2.0 ** (-span - 1.0))) + span) * (CODES / span) + 1.5
    return jnp.clip(position, 0.0, 65535.0).astype(jnp.int32)


def opacity_terms(largest):
    half = 0.5 * largest
    nodes = [half + half * math.cos(math.pi * (2 * i + 1) / 6.0) for i in range(3)]
    values = [-math.expm1(-y) / y for y in nodes]
    c0, c1, c2 = (float(c) for c in np.polynomial.polynomial.polyfit(nodes, values, 2))
    k = c2 ** (1.0 / 3.0)
    a = c1 / (2.0 * k * k)
    return k, a, c0 / k - a * a


def full(x):
    return jnp.full((SUB, LANES), x, jnp.float32)


def lanes_of(t):
    return slice(t * LANES, (t + 1) * LANES)


def lane_index():
    return lax.broadcasted_iota(jnp.int32, (SUB, LANES), 1)


def is_even(axis):
    return lax.rem(lax.axis_index(axis), 2) == 0


def edges_kernel(x_low, x_high, y_low, y_high, z_low, z_high, x_first, x_second, y_out, z_first, z_second, rows_x):
    depth = x_low.shape[0]
    even_x, even_z = is_even("gx"), is_even("gz")
    for z in range(depth):
        low = x_low[z].astype(jnp.float32)
        high = x_high[z].astype(jnp.float32)
        rows_x[0, z:z + 1, :] = low[:1]
        rows_x[1, z:z + 1, :] = high[15:]
    top, bottom = rows_x[0], rows_x[1]
    x_first[...] = jnp.where(even_x, bottom, top).astype(x_first.dtype)
    x_second[...] = jnp.where(even_x, top, bottom).astype(x_second.dtype)
    lane = lane_index()
    for i in range(y_low.shape[1] // 16):
        sides = [jnp.zeros((SUB, LANES), jnp.float32)] * 2
        for z in range(depth):
            low = y_low[z, 16 * i:16 * i + 16, :].astype(jnp.float32)
            high = y_high[z, 16 * i:16 * i + 16, :].astype(jnp.float32)
            for part in range(2):
                at = slice(8 * part, 8 * part + 8)
                sides[part] = jnp.where(lane == z, low[at, :1], sides[part])
                sides[part] = jnp.where(lane == depth + z, high[at, LANES - 1:], sides[part])
        for part in range(2):
            y_out[pl.ds(2 * i + part, SUB, stride=GROUPS), :] = sides[part]

    @pl.when(even_z)
    def _():
        z_first[...] = z_high[0]
        z_second[...] = z_low[0]

    @pl.when(jnp.logical_not(even_z))
    def _():
        z_first[...] = z_low[0]
        z_second[...] = z_high[0]


def slots_of(i):
    return pl.ds(i, SUB, stride=PITCH)


def spread_kernel(knots_ref, colour_ref, density_ref, vol_ref, cells, grads, consts, *, depth_total):
    depth, rows, cols = vol_ref.shape
    lane = lax.broadcasted_iota(jnp.int32, (16, LANES), 1)
    tiles = cols // LANES
    prepare(consts, knots_ref, colour_ref, density_ref, depth_total)

    def step(z, carry):
        for c in range(rows // 16):
            plane = vol_ref[z, 16 * c:16 * c + 16, :].astype(jnp.float32)
            left = pltpu.roll(plane, 1, 1)
            right = pltpu.roll(plane, cols - 1, 1)
            for t in range(tiles):
                l, r = left[:, lanes_of(t)], right[:, lanes_of(t)]
                if t == 0:
                    l = jnp.where(lane == 0, 0.0, l)
                if t == tiles - 1:
                    r = jnp.where(lane == LANES - 1, 0.0, r)
                across = r - l
                own = plane[:, lanes_of(t)]
                for part in range(2):
                    at = slice(8 * part, 8 * part + 8)
                    cells[t, z, slots_of(2 * c + part), :] = own[at]
                    grads[t, z, slots_of(2 * c + part), :] = across[at]
        return carry

    lax.fori_loop(0, depth, step, 0)


def prepare(consts, knots_ref, colour_ref, density_ref, depth_total):
    top = BINS - 1.0
    slants = []
    for k in range(SEGMENTS):
        low = full(knots_ref[k].astype(jnp.float32))
        high = full(knots_ref[k + 1].astype(jnp.float32))
        slants.append(top / (high - low))
        if k:
            consts[k - 1] = low * (1.0 / top)
    unit = opacity_terms(10.0 / depth_total)[0] / depth_total
    consts[6] = full(density_ref[0]) * unit
    for k in range(SEGMENTS):
        step = full(density_ref[k + 1]) - full(density_ref[k])
        consts[7 + k] = step * unit * slants[k]
    for c in range(3):
        scale = full(colour_scale(colour_ref, c))
        consts[SCALES + c] = scale
        unscale = DIFFUSE / scale
        consts[14 + 8 * c] = full(colour_ref[c, 0]) * unscale
        for k in range(SEGMENTS):
            step = full(colour_ref[c, k + 1]) - full(colour_ref[c, k])
            consts[15 + 8 * c + k] = step * unscale * slants[k]


def composite(consts, cell, grad_x, grad_y, depth, depth_total):
    _, shift, rest = opacity_terms(10.0 / depth_total)
    points = [consts[k] for k in range(6)]
    first = consts[6]
    slopes = [consts[7 + k] for k in range(SEGMENTS)]
    transmit = jnp.ones((SUB, LANES), jnp.float32)
    weight = None
    moments = None
    earlier, now = cell(-1), cell(0)
    for z in range(depth):
        later = cell(z + 1)
        gx, gy, gz = grad_x(z), grad_y(z), later - earlier
        across = gy + gz
        facing = jnp.abs(gx + (across + across))
        shading = AMBIENT / DIFFUSE + facing * lax.rsqrt(gx * gx + gy * gy + (gz * gz + 1.0))
        capped = [jnp.minimum(now, p) for p in points] + [now]
        ramps = [capped[0]] + [capped[k + 1] - capped[k] for k in range(6)]
        y = first
        for k in range(SEGMENTS):
            y = y + ramps[k] * slopes[k]
        shifted = y + shift
        taken = transmit * (y * (shifted * shifted + rest))
        transmit = transmit - taken
        shaded = taken * shading
        if z == 0:
            weight = shaded
            moments = [shaded * r for r in ramps]
        else:
            weight = weight + shaded
            moments = [m + shaded * r for m, r in zip(moments, ramps)]
        earlier, now = now, later
    values = []
    for c in range(3):
        value = weight * consts[14 + 8 * c]
        for k in range(SEGMENTS):
            value = value + moments[k] * consts[15 + 8 * c + k]
        values.append(value)
    return values + [1.0 - transmit]


def spread_side(ref, sides, side):
    for c in range(ref.shape[0] // 16):
        plane = ref[16 * c:16 * c + 16, :].astype(jnp.float32)
        for t in range(sides.shape[1]):
            for part in range(2):
                sides[side, t, slots_of(2 * c + part), :] = plane[8 * part:8 * part + 8, lanes_of(t)]


def place_edges(cells, grads, x_first, x_second, y_before, y_after, parity):
    tiles, depth = cells.shape[:2]
    slot = jnp.where(parity == 0, ABOVE, BELOW)
    second = (parity == 0) == is_even("gx")
    edge = jnp.where(second, x_second[...].astype(jnp.float32), x_first[...].astype(jnp.float32))
    for z in range(depth):
        for t in range(tiles):
            cells[t, z, pl.ds(slot, 1), :] = edge[z:z + 1, lanes_of(t)]
    lane = lane_index()

    def step(j, carry):
        r = 4 * parity + j
        rows = pl.ds(pl.multiple_of(SUB * r, SUB), SUB)
        at = pl.ds(PITCH * r, SUB)
        before, after = y_before[rows, :], y_after[rows, :]
        for z in range(depth):
            first = jnp.where(lane == 0, before[:, depth + z:depth + z + 1], 0.0)
            last = jnp.where(lane == LANES - 1, after[:, z:z + 1], 0.0)
            grads[0, z, at, :] = grads[0, z, at, :] - first
            grads[tiles - 1, z, at, :] = grads[tiles - 1, z, at, :] + last
        return carry

    lax.fori_loop(0, 4, step, 0)


def half_loop(consts, cells, grads, sides, parity, depth_total, store):
    tiles, depth = cells.shape[:2]

    def work(t, j):
        r = 4 * parity + j
        at = pl.ds(PITCH * r, SUB)
        above = pl.ds(jnp.where(r == 0, ABOVE, PITCH * r - PITCH), SUB)
        below = pl.ds(jnp.where(r == GROUPS - 1, 1, PITCH * r + PITCH), SUB)

        def cell(z):
            if z < 0:
                return sides[0, t, at, :]
            if z == depth:
                return sides[1, t, at, :]
            return cells[t, z, at, :]

        values = composite(
            consts,
            cell,
            lambda z: cells[t, z, below, :] - cells[t, z, above, :],
            lambda z: grads[t, z, at, :],
            depth,
            depth_total,
        )
        store(t, j, values)

    def step(n, carry):
        t, j = n // 2, 2 * (n % 2)
        work(t, j)
        work(t, j + 1)
        return carry

    lax.fori_loop(0, 2 * tiles, step, 0)


def pack(values):
    codes = [encode(v, COLOUR_SPAN) for v in values[:3]] + [encode(values[3], COVER_SPAN)]
    return codes[0] | (codes[1] << 16), codes[2] | (codes[3] << 16)


def decode(code, span):
    value = jnp.exp2(code.astype(jnp.float32) * (span / CODES) - (span + span / CODES))
    return jnp.where(code > 0, value, 0.0)


def my_parity():
    return lax.rem(lax.axis_index("gz"), 2)


def theirs_kernel(
    consts, cells_in, grads_in, x_first, x_second, y_before, y_after, z_first, z_second,
    out_ref, cells, grads, sides, *, depth_total,
):
    parity = 1 - my_parity()
    before = jnp.where(is_even("gz"), 1, 0)
    spread_side(z_first, sides, before)
    spread_side(z_second, sides, 1 - before)
    place_edges(cells, grads, x_first, x_second, y_before, y_after, parity)

    def store(t, j, values):
        first, second = pack(values)
        out_ref[j, t] = first
        out_ref[4 + j, t] = second

    half_loop(consts, cells, grads, sides, parity, depth_total, store)


def ours_kernel(
    consts, cells_in, grads_in, x_first, x_second, y_before, y_after, sides,
    out_ref, cells, grads, *, depth_total,
):
    parity = my_parity()
    place_edges(cells, grads, x_first, x_second, y_before, y_after, parity)

    def store(t, j, values):
        for c in range(4):
            out_ref[4 * c + j, t] = values[c]

    half_loop(consts, cells, grads, sides, parity, depth_total, store)


def pair_kernel(ours_ref, theirs_ref, out_ref):
    tiles = ours_ref.shape[1]
    front = lax.rem(lax.axis_index("gz"), 2) == 0

    def step(t, carry):
        for j in range(4):
            ours = [ours_ref[4 * c + j, t] for c in range(4)]
            first, second = theirs_ref[j, t], theirs_ref[4 + j, t]
            theirs = [
                decode(first & 0xFFFF, COLOUR_SPAN),
                decode(lax.shift_right_logical(first, 16), COLOUR_SPAN),
                decode(second & 0xFFFF, COLOUR_SPAN),
                decode(lax.shift_right_logical(second, 16), COVER_SPAN),
            ]
            keep_ours = jnp.where(front, 1.0, 1.0 - theirs[3])
            keep_theirs = jnp.where(front, 1.0 - ours[3], 1.0)
            words = pack([o * keep_ours + p * keep_theirs for o, p in zip(ours, theirs)])
            for w in range(2):
                out_ref[pl.ds(t * SUB + 4 * w + j, SUB, stride=tiles * SUB), :] = words[w]
        return carry

    lax.fori_loop(0, tiles, step, 0)


def compose_kernel(consts, pieces_ref, image_ref, coverage_ref):
    count = pieces_ref.shape[0]
    low_rows = lax.broadcasted_iota(jnp.int32, (SUB, LANES), 0) < 4
    scales = [consts[SCALES + c] for c in range(3)]
    step = COLOUR_SPAN / CODES
    steps_hi = jnp.where(low_rows, step, COVER_SPAN / CODES)
    start_hi = jnp.where(low_rows, -COLOUR_SPAN - step, -COVER_SPAN - COVER_SPAN / CODES)

    def level(code, steps, start):
        value = jnp.exp2(code.astype(jnp.float32) * steps + start)
        return jnp.where(code > 0, value, 0.0)

    for t in range(pieces_ref.shape[1] // SUB):
        low = high = None
        transmit = None
        for piece in range(count):
            word = pieces_ref[piece, t * SUB:(t + 1) * SUB, :]
            red_blue = level(word & 0xFFFF, step, -COLOUR_SPAN - step)
            green_cover = level(lax.shift_right_logical(word, 16), steps_hi, start_hi)
            cover = jnp.where(low_rows, pltpu.roll(green_cover, 4, 0), green_cover)
            if piece == 0:
                low, high, transmit = red_blue, green_cover, 1.0 - cover
            else:
                low = low + transmit * red_blue
                high = high + transmit * green_cover
                transmit = transmit * (1.0 - cover)
        low = low * jnp.where(low_rows, scales[0], scales[2])
        high = high * jnp.where(low_rows, scales[1], 1.0)
        image_ref[0, :, lanes_of(t)] = low[:4]
        image_ref[1, :, lanes_of(t)] = high[:4]
        image_ref[2, :, lanes_of(t)] = low[4:]
        coverage_ref[:, lanes_of(t)] = high[4:]


def meet(first, second, axis):
    count = lax.axis_size(axis)

    def swap(edge, start):
        pairs = [(i, i + 1) for i in range(start, count - 1, 2)]
        return lax.ppermute(edge, axis, pairs + [(j, i) for i, j in pairs])

    return swap(first, 0), swap(second, 1)


def shift_both(edges, axis):
    count = lax.axis_size(axis)
    up = [(i, i + 1) for i in range(count - 1)]
    down = [(j, i) for i, j in up]
    return lax.ppermute(edges, axis, up), lax.ppermute(edges, axis, down)


def cost(flops, moved):
    return pl.CostEstimate(flops=flops, bytes_accessed=moved, transcendentals=0)


def on_device(volume, knot_bins, tf_colour, tf_density):
    depth, rows, cols = volume.shape
    count = lax.axis_size("gz")
    tiles = cols // LANES
    depth_total = float(depth * count)
    smem = pl.BlockSpec(memory_space=pltpu.SMEM)
    vmem = pl.BlockSpec(memory_space=pltpu.VMEM)
    params = pltpu.CompilerParams(vmem_limit_bytes=24 << 20)
    f32 = jnp.float32

    def whole(*shape):
        return pl.BlockSpec(shape, lambda n: (0,) * len(shape))

    x_first, x_second, y_edges, z_first, z_second = pl.pallas_call(
        edges_kernel,
        grid=(1,),
        out_shape=(
            jax.ShapeDtypeStruct((depth, cols), volume.dtype),
            jax.ShapeDtypeStruct((depth, cols), volume.dtype),
            jax.ShapeDtypeStruct((rows, LANES), f32),
            jax.ShapeDtypeStruct((rows, cols), volume.dtype),
            jax.ShapeDtypeStruct((rows, cols), volume.dtype),
        ),
        in_specs=[
            pl.BlockSpec((depth, 16, cols), lambda n: (0, 0, 0)),
            pl.BlockSpec((depth, 16, cols), lambda n: (0, rows // 16 - 1, 0)),
            pl.BlockSpec((depth, rows, LANES), lambda n: (0, 0, 0)),
            pl.BlockSpec((depth, rows, LANES), lambda n: (0, 0, tiles - 1)),
            pl.BlockSpec((1, rows, cols), lambda n: (0, 0, 0)),
            pl.BlockSpec((1, rows, cols), lambda n: (depth - 1, 0, 0)),
        ],
        out_specs=(whole(depth, cols), whole(depth, cols), whole(rows, LANES), whole(rows, cols), whole(rows, cols)),
        scratch_shapes=[pltpu.VMEM((2, depth, cols), f32)],
        compiler_params=params,
        cost_estimate=cost(1 << 20, 2 << 20),
        name="edges",
    )(*[volume] * 6)
    z_got = meet(z_first, z_second, "gz")
    y_got = shift_both(y_edges, "gy")
    x_got = meet(x_first, x_second, "gx")
    spread_shape = jax.ShapeDtypeStruct((tiles, depth, PITCH * GROUPS, LANES), f32)
    consts_shape = jax.ShapeDtypeStruct((SCALES + 3, SUB, LANES), f32)
    cells, grads, consts = pl.pallas_call(
        functools.partial(spread_kernel, depth_total=depth_total),
        out_shape=(spread_shape, spread_shape, consts_shape),
        in_specs=[smem] * 3 + [vmem],
        out_specs=(vmem,) * 3,
        compiler_params=params,
        cost_estimate=cost(1 << 23, 2 << 20),
        name="spread",
    )(knot_bins, tf_colour, tf_density, volume)
    work = cost(1 << 26, 1 << 23)
    theirs, cells, grads, sides = pl.pallas_call(
        functools.partial(theirs_kernel, depth_total=depth_total),
        out_shape=(
            jax.ShapeDtypeStruct((8, tiles, SUB, LANES), jnp.int32),
            spread_shape,
            spread_shape,
            jax.ShapeDtypeStruct((2, tiles, PITCH * GROUPS, LANES), f32),
        ),
        in_specs=[vmem] * 9,
        out_specs=(vmem,) * 4,
        input_output_aliases={1: 1, 2: 2},
        compiler_params=params,
        cost_estimate=work,
        name="theirs",
    )(consts, cells, grads, *x_got, *y_got, *z_got)
    arrived = lax.ppermute(theirs, "gz", [(i, i ^ 1) for i in range(count)])
    ours, _, _ = pl.pallas_call(
        functools.partial(ours_kernel, depth_total=depth_total),
        out_shape=(jax.ShapeDtypeStruct((16, tiles, SUB, LANES), f32), spread_shape, spread_shape),
        in_specs=[vmem] * 8,
        out_specs=(vmem,) * 3,
        input_output_aliases={1: 1, 2: 2},
        compiler_params=params,
        cost_estimate=work,
        name="ours",
    )(consts, cells, grads, *x_got, *y_got, sides)
    half = count // 2
    codes = pl.pallas_call(
        pair_kernel,
        out_shape=jax.ShapeDtypeStruct((half * tiles * SUB, LANES), jnp.int32),
        in_specs=[vmem] * 2,
        out_specs=vmem,
        compiler_params=params,
        name="pair",
    )(ours, arrived)
    pieces = lax.all_to_all(
        codes.reshape(half, tiles * SUB, LANES),
        "gz",
        split_axis=0,
        concat_axis=0,
        tiled=True,
        axis_index_groups=[[2 * i + e for i in range(half)] for e in range(2)],
    )
    band = rows // count
    return pl.pallas_call(
        compose_kernel,
        out_shape=(
            jax.ShapeDtypeStruct((3, band, cols), f32),
            jax.ShapeDtypeStruct((band, cols), f32),
        ),
        in_specs=[vmem, vmem],
        out_specs=(vmem, vmem),
        name="compose",
    )(consts, pieces)


def solution(mesh):
    placed = (P("gz", "gx", "gy"), P(), P(), P())
    return jax.shard_map(
        on_device,
        mesh=mesh,
        in_specs=placed,
        out_specs=(P(None, ("gx", "gz"), "gy"), P(("gx", "gz"), "gy")),
        check_vma=False,
    )
```

```python
import functools
import math

import jax
import jax.numpy as jnp
import numpy as np
from jax import lax
from jax.experimental import pallas as pl
from jax.experimental.pallas import tpu as pltpu
from jax.sharding import PartitionSpec as P

BINS = 256
KNOTS = 8
SEGMENTS = KNOTS - 1
AMBIENT = 0.2
DIFFUSE = (1.0 - AMBIENT) / 3.0
LANES = 128
SUB = 8
GROUPS = 8
PITCH = 9
ABOVE = PITCH * (GROUPS - 1) - 1
BELOW = GROUPS
SCALES = 38

COLOUR_SPAN = 26.0
COVER_SPAN = 9.0
CODES = 65534.0


def colour_scale(colour_ref, channel):
    largest = colour_ref[channel, 0]
    for k in range(1, KNOTS):
        largest = jnp.maximum(largest, colour_ref[channel, k])
    return jnp.maximum(largest, 1e-30)


def encode(value, span):
    position = (jnp.log2(jnp.maximum(value, 2.0 ** (-span - 1.0))) + span) * (CODES / span) + 1.5
    return jnp.clip(position, 0.0, 65535.0).astype(jnp.int32)


def opacity_terms(largest):
    half = 0.5 * largest
    nodes = [half + half * math.cos(math.pi * (2 * i + 1) / 6.0) for i in range(3)]
    values = [-math.expm1(-y) / y for y in nodes]
    c0, c1, c2 = (float(c) for c in np.polynomial.polynomial.polyfit(nodes, values, 2))
    k = c2 ** (1.0 / 3.0)
    a = c1 / (2.0 * k * k)
    return k, a, c0 / k - a * a


def full(x):
    return jnp.full((SUB, LANES), x, jnp.float32)


def lanes_of(t):
    return slice(t * LANES, (t + 1) * LANES)


def lane_index():
    return lax.broadcasted_iota(jnp.int32, (SUB, LANES), 1)


def is_even(axis):
    return lax.rem(lax.axis_index(axis), 2) == 0


def edges_kernel(x_low, x_high, y_low, y_high, z_low, z_high, x_first, x_second, y_out, z_first, z_second, rows_x, cols_y):
    depth = x_low.shape[0]
    even_x, even_z = is_even("gx"), is_even("gz")
    for z in range(depth):
        low = x_low[z].astype(jnp.float32)
        high = x_high[z].astype(jnp.float32)
        rows_x[0, z:z + 1, :] = low[:1]
        rows_x[1, z:z + 1, :] = high[15:]
    top, bottom = rows_x[0], rows_x[1]
    x_first[...] = jnp.where(even_x, bottom, top).astype(x_first.dtype)
    x_second[...] = jnp.where(even_x, top, bottom).astype(x_second.dtype)
    lane = lane_index()
    for i in range(y_low.shape[1] // 16):
        sides = [jnp.zeros((SUB, LANES), jnp.float32)] * 2
        for z in range(depth):
            low = y_low[z, 16 * i:16 * i + 16, :].astype(jnp.float32)
            high = y_high[z, 16 * i:16 * i + 16, :].astype(jnp.float32)
            for part in range(2):
                at = slice(8 * part, 8 * part + 8)
                sides[part] = jnp.where(lane == z, low[at, :1], sides[part])
                sides[part] = jnp.where(lane == depth + z, high[at, LANES - 1:], sides[part])
        for part in range(2):
            cols_y[pl.ds(2 * i + part, SUB, stride=GROUPS), :] = sides[part]
    y_out[...] = cols_y[...].astype(y_out.dtype)

    @pl.when(even_z)
    def _():
        z_first[...] = z_high[0]
        z_second[...] = z_low[0]

    @pl.when(jnp.logical_not(even_z))
    def _():
        z_first[...] = z_low[0]
        z_second[...] = z_high[0]


def slots_of(i):
    return pl.ds(i, SUB, stride=PITCH)


def spread_kernel(knots_ref, colour_ref, density_ref, vol_ref, cells, grads, consts, *, depth_total):
    depth, rows, cols = vol_ref.shape
    lane = lax.broadcasted_iota(jnp.int32, (16, LANES), 1)
    tiles = cols // LANES
    prepare(consts, knots_ref, colour_ref, density_ref, depth_total)

    def step(z, carry):
        for c in range(rows // 16):
            plane = vol_ref[z, 16 * c:16 * c + 16, :].astype(jnp.float32)
            left = pltpu.roll(plane, 1, 1)
            right = pltpu.roll(plane, cols - 1, 1)
            for t in range(tiles):
                l, r = left[:, lanes_of(t)], right[:, lanes_of(t)]
                if t == 0:
                    l = jnp.where(lane == 0, 0.0, l)
                if t == tiles - 1:
                    r = jnp.where(lane == LANES - 1, 0.0, r)
                across = r - l
                own = plane[:, lanes_of(t)]
                for part in range(2):
                    at = slice(8 * part, 8 * part + 8)
                    cells[t, z, slots_of(2 * c + part), :] = own[at]
                    grads[t, z, slots_of(2 * c + part), :] = across[at]
        return carry

    lax.fori_loop(0, depth, step, 0)


def prepare(consts, knots_ref, colour_ref, density_ref, depth_total):
    top = BINS - 1.0
    slants = []
    for k in range(SEGMENTS):
        low = full(knots_ref[k].astype(jnp.float32))
        high = full(knots_ref[k + 1].astype(jnp.float32))
        slants.append(top / (high - low))
        if k:
            consts[k - 1] = low * (1.0 / top)
    unit = opacity_terms(10.0 / depth_total)[0] / depth_total
    consts[6] = full(density_ref[0]) * unit
    for k in range(SEGMENTS):
        step = full(density_ref[k + 1]) - full(density_ref[k])
        consts[7 + k] = step * unit * slants[k]
    for c in range(3):
        scale = full(colour_scale(colour_ref, c))
        consts[SCALES + c] = scale
        unscale = DIFFUSE / scale
        consts[14 + 8 * c] = full(colour_ref[c, 0]) * unscale
        for k in range(SEGMENTS):
            step = full(colour_ref[c, k + 1]) - full(colour_ref[c, k])
            consts[15 + 8 * c + k] = step * unscale * slants[k]


def composite(consts, cell, grad_x, grad_y, depth, depth_total):
    _, shift, rest = opacity_terms(10.0 / depth_total)
    points = [consts[k] for k in range(6)]
    first = consts[6]
    slopes = [consts[7 + k] for k in range(SEGMENTS)]
    transmit = jnp.ones((SUB, LANES), jnp.float32)
    weight = None
    moments = None
    earlier, now = cell(-1), cell(0)
    for z in range(depth):
        later = cell(z + 1)
        gx, gy, gz = grad_x(z), grad_y(z), later - earlier
        across = gy + gz
        facing = jnp.abs(gx + (across + across))
        shading = AMBIENT / DIFFUSE + facing * lax.rsqrt(gx * gx + gy * gy + (gz * gz + 1.0))
        capped = [jnp.minimum(now, p) for p in points] + [now]
        ramps = [capped[0]] + [capped[k + 1] - capped[k] for k in range(6)]
        y = first
        for k in range(SEGMENTS):
            y = y + ramps[k] * slopes[k]
        shifted = y + shift
        taken = transmit * (y * (shifted * shifted + rest))
        transmit = transmit - taken
        shaded = taken * shading
        if z == 0:
            weight = shaded
            moments = [shaded * r for r in ramps]
        else:
            weight = weight + shaded
            moments = [m + shaded * r for m, r in zip(moments, ramps)]
        earlier, now = now, later
    values = []
    for c in range(3):
        value = weight * consts[14 + 8 * c]
        for k in range(SEGMENTS):
            value = value + moments[k] * consts[15 + 8 * c + k]
        values.append(value)
    return values + [1.0 - transmit]


def spread_side(ref, sides, side):
    for c in range(ref.shape[0] // 16):
        plane = ref[16 * c:16 * c + 16, :].astype(jnp.float32)
        for t in range(sides.shape[1]):
            for part in range(2):
                sides[side, t, slots_of(2 * c + part), :] = plane[8 * part:8 * part + 8, lanes_of(t)]


def place_edges(cells, grads, x_first, x_second, y_before, y_after, columns, parity):
    tiles, depth = cells.shape[:2]
    slot = jnp.where(parity == 0, ABOVE, BELOW)
    columns[0] = y_before[...].astype(jnp.float32)
    columns[1] = y_after[...].astype(jnp.float32)
    second = (parity == 0) == is_even("gx")
    edge = jnp.where(second, x_second[...].astype(jnp.float32), x_first[...].astype(jnp.float32))
    for z in range(depth):
        for t in range(tiles):
            cells[t, z, pl.ds(slot, 1), :] = edge[z:z + 1, lanes_of(t)]
    lane = lane_index()

    def step(j, carry):
        r = 4 * parity + j
        rows = pl.ds(pl.multiple_of(SUB * r, SUB), SUB)
        at = pl.ds(PITCH * r, SUB)
        before, after = columns[0, rows, :], columns[1, rows, :]
        for z in range(depth):
            first = jnp.where(lane == 0, before[:, depth + z:depth + z + 1], 0.0)
            last = jnp.where(lane == LANES - 1, after[:, z:z + 1], 0.0)
            grads[0, z, at, :] = grads[0, z, at, :] - first
            grads[tiles - 1, z, at, :] = grads[tiles - 1, z, at, :] + last
        return carry

    lax.fori_loop(0, 4, step, 0)


def half_loop(consts, cells, grads, sides, parity, depth_total, store):
    tiles, depth = cells.shape[:2]

    def work(t, j):
        r = 4 * parity + j
        at = pl.ds(PITCH * r, SUB)
        above = pl.ds(jnp.where(r == 0, ABOVE, PITCH * r - PITCH), SUB)
        below = pl.ds(jnp.where(r == GROUPS - 1, 1, PITCH * r + PITCH), SUB)

        def cell(z):
            if z < 0:
                return sides[0, t, at, :]
            if z == depth:
                return sides[1, t, at, :]
            return cells[t, z, at, :]

        values = composite(
            consts,
            cell,
            lambda z: cells[t, z, below, :] - cells[t, z, above, :],
            lambda z: grads[t, z, at, :],
            depth,
            depth_total,
        )
        store(t, j, values)

    def step(n, carry):
        t, j = n // 2, 2 * (n % 2)
        work(t, j)
        work(t, j + 1)
        return carry

    lax.fori_loop(0, 2 * tiles, step, 0)


def pack(values):
    codes = [encode(v, COLOUR_SPAN) for v in values[:3]] + [encode(values[3], COVER_SPAN)]
    return codes[0] | (codes[1] << 16), codes[2] | (codes[3] << 16)


def decode(code, span):
    value = jnp.exp2(code.astype(jnp.float32) * (span / CODES) - (span + span / CODES))
    return jnp.where(code > 0, value, 0.0)


def my_parity():
    return lax.rem(lax.axis_index("gz"), 2)


def theirs_kernel(
    consts, cells_in, grads_in, x_first, x_second, y_before, y_after, z_first, z_second,
    out_ref, cells, grads, sides, columns, *, depth_total,
):
    parity = 1 - my_parity()
    before = jnp.where(is_even("gz"), 1, 0)
    spread_side(z_first, sides, before)
    spread_side(z_second, sides, 1 - before)
    place_edges(cells, grads, x_first, x_second, y_before, y_after, columns, parity)

    def store(t, j, values):
        first, second = pack(values)
        out_ref[j, t] = first
        out_ref[4 + j, t] = second

    half_loop(consts, cells, grads, sides, parity, depth_total, store)


def ours_kernel(
    consts, cells_in, grads_in, x_first, x_second, y_before, y_after, sides,
    out_ref, cells, grads, columns, *, depth_total,
):
    parity = my_parity()
    place_edges(cells, grads, x_first, x_second, y_before, y_after, columns, parity)

    def store(t, j, values):
        for c in range(4):
            out_ref[4 * c + j, t] = values[c]

    half_loop(consts, cells, grads, sides, parity, depth_total, store)


def pair_kernel(ours_ref, theirs_ref, out_ref):
    tiles = ours_ref.shape[1]
    front = lax.rem(lax.axis_index("gz"), 2) == 0

    def step(t, carry):
        for j in range(4):
            ours = [ours_ref[4 * c + j, t] for c in range(4)]
            first, second = theirs_ref[j, t], theirs_ref[4 + j, t]
            theirs = [
                decode(first & 0xFFFF, COLOUR_SPAN),
                decode(lax.shift_right_logical(first, 16), COLOUR_SPAN),
                decode(second & 0xFFFF, COLOUR_SPAN),
                decode(lax.shift_right_logical(second, 16), COVER_SPAN),
            ]
            keep_ours = jnp.where(front, 1.0, 1.0 - theirs[3])
            keep_theirs = jnp.where(front, 1.0 - ours[3], 1.0)
            words = pack([o * keep_ours + p * keep_theirs for o, p in zip(ours, theirs)])
            for w in range(2):
                out_ref[pl.ds(t * SUB + 4 * w + j, SUB, stride=tiles * SUB), :] = words[w]
        return carry

    lax.fori_loop(0, tiles, step, 0)


def compose_kernel(consts, pieces_ref, image_ref, coverage_ref):
    count = pieces_ref.shape[0]
    low_rows = lax.broadcasted_iota(jnp.int32, (SUB, LANES), 0) < 4
    scales = [consts[SCALES + c] for c in range(3)]
    step = COLOUR_SPAN / CODES
    steps_hi = jnp.where(low_rows, step, COVER_SPAN / CODES)
    start_hi = jnp.where(low_rows, -COLOUR_SPAN - step, -COVER_SPAN - COVER_SPAN / CODES)

    def level(code, steps, start):
        value = jnp.exp2(code.astype(jnp.float32) * steps + start)
        return jnp.where(code > 0, value, 0.0)

    for t in range(pieces_ref.shape[1] // SUB):
        low = high = None
        transmit = None
        for piece in range(count):
            word = pieces_ref[piece, t * SUB:(t + 1) * SUB, :]
            red_blue = level(word & 0xFFFF, step, -COLOUR_SPAN - step)
            green_cover = level(lax.shift_right_logical(word, 16), steps_hi, start_hi)
            cover = jnp.where(low_rows, pltpu.roll(green_cover, 4, 0), green_cover)
            if piece == 0:
                low, high, transmit = red_blue, green_cover, 1.0 - cover
            else:
                low = low + transmit * red_blue
                high = high + transmit * green_cover
                transmit = transmit * (1.0 - cover)
        low = low * jnp.where(low_rows, scales[0], scales[2])
        high = high * jnp.where(low_rows, scales[1], 1.0)
        image_ref[0, :, lanes_of(t)] = low[:4]
        image_ref[1, :, lanes_of(t)] = high[:4]
        image_ref[2, :, lanes_of(t)] = low[4:]
        coverage_ref[:, lanes_of(t)] = high[4:]


def meet(first, second, axis):
    count = lax.axis_size(axis)

    def swap(edge, start):
        pairs = [(i, i + 1) for i in range(start, count - 1, 2)]
        return lax.ppermute(edge, axis, pairs + [(j, i) for i, j in pairs])

    return swap(first, 0), swap(second, 1)


def shift_both(edges, axis):
    count = lax.axis_size(axis)
    up = [(i, i + 1) for i in range(count - 1)]
    down = [(j, i) for i, j in up]
    return lax.ppermute(edges, axis, up), lax.ppermute(edges, axis, down)


def cost(flops, moved):
    return pl.CostEstimate(flops=flops, bytes_accessed=moved, transcendentals=0)


def on_device(volume, knot_bins, tf_colour, tf_density):
    depth, rows, cols = volume.shape
    count = lax.axis_size("gz")
    tiles = cols // LANES
    depth_total = float(depth * count)
    smem = pl.BlockSpec(memory_space=pltpu.SMEM)
    vmem = pl.BlockSpec(memory_space=pltpu.VMEM)
    params = pltpu.CompilerParams(vmem_limit_bytes=24 << 20)
    f32 = jnp.float32

    def whole(*shape):
        return pl.BlockSpec(shape, lambda n: (0,) * len(shape))

    x_first, x_second, y_edges, z_first, z_second = pl.pallas_call(
        edges_kernel,
        grid=(1,),
        out_shape=(
            jax.ShapeDtypeStruct((depth, cols), volume.dtype),
            jax.ShapeDtypeStruct((depth, cols), volume.dtype),
            jax.ShapeDtypeStruct((rows, LANES), volume.dtype),
            jax.ShapeDtypeStruct((rows, cols), volume.dtype),
            jax.ShapeDtypeStruct((rows, cols), volume.dtype),
        ),
        in_specs=[
            pl.BlockSpec((depth, 16, cols), lambda n: (0, 0, 0)),
            pl.BlockSpec((depth, 16, cols), lambda n: (0, rows // 16 - 1, 0)),
            pl.BlockSpec((depth, rows, LANES), lambda n: (0, 0, 0)),
            pl.BlockSpec((depth, rows, LANES), lambda n: (0, 0, tiles - 1)),
            pl.BlockSpec((1, rows, cols), lambda n: (0, 0, 0)),
            pl.BlockSpec((1, rows, cols), lambda n: (depth - 1, 0, 0)),
        ],
        out_specs=(whole(depth, cols), whole(depth, cols), whole(rows, LANES), whole(rows, cols), whole(rows, cols)),
        scratch_shapes=[pltpu.VMEM((2, depth, cols), f32), pltpu.VMEM((rows, LANES), f32)],
        compiler_params=params,
        cost_estimate=cost(1 << 20, 2 << 20),
        name="edges",
    )(*[volume] * 6)
    z_got = meet(z_first, z_second, "gz")
    y_got = shift_both(y_edges, "gy")
    x_got = meet(x_first, x_second, "gx")
    spread_shape = jax.ShapeDtypeStruct((tiles, depth, PITCH * GROUPS, LANES), f32)
    consts_shape = jax.ShapeDtypeStruct((SCALES + 3, SUB, LANES), f32)
    cells, grads, consts = pl.pallas_call(
        functools.partial(spread_kernel, depth_total=depth_total),
        out_shape=(spread_shape, spread_shape, consts_shape),
        in_specs=[smem] * 3 + [vmem],
        out_specs=(vmem,) * 3,
        compiler_params=params,
        cost_estimate=cost(1 << 23, 2 << 20),
        name="spread",
    )(knot_bins, tf_colour, tf_density, volume)
    work = cost(1 << 26, 1 << 23)
    theirs, cells, grads, sides = pl.pallas_call(
        functools.partial(theirs_kernel, depth_total=depth_total),
        out_shape=(
            jax.ShapeDtypeStruct((8, tiles, SUB, LANES), jnp.int32),
            spread_shape,
            spread_shape,
            jax.ShapeDtypeStruct((2, tiles, PITCH * GROUPS, LANES), f32),
        ),
        in_specs=[vmem] * 9,
        out_specs=(vmem,) * 4,
        input_output_aliases={1: 1, 2: 2},
        scratch_shapes=[pltpu.VMEM((2, rows, LANES), f32)],
        compiler_params=params,
        cost_estimate=work,
        name="theirs",
    )(consts, cells, grads, *x_got, *y_got, *z_got)
    arrived = lax.ppermute(theirs, "gz", [(i, i ^ 1) for i in range(count)])
    ours, _, _ = pl.pallas_call(
        functools.partial(ours_kernel, depth_total=depth_total),
        out_shape=(jax.ShapeDtypeStruct((16, tiles, SUB, LANES), f32), spread_shape, spread_shape),
        in_specs=[vmem] * 8,
        out_specs=(vmem,) * 3,
        input_output_aliases={1: 1, 2: 2},
        scratch_shapes=[pltpu.VMEM((2, rows, LANES), f32)],
        compiler_params=params,
        cost_estimate=work,
        name="ours",
    )(consts, cells, grads, *x_got, *y_got, sides)
    half = count // 2
    codes = pl.pallas_call(
        pair_kernel,
        out_shape=jax.ShapeDtypeStruct((half * tiles * SUB, LANES), jnp.int32),
        in_specs=[vmem] * 2,
        out_specs=vmem,
        compiler_params=params,
        name="pair",
    )(ours, arrived)
    pieces = lax.all_to_all(
        codes.reshape(half, tiles * SUB, LANES),
        "gz",
        split_axis=0,
        concat_axis=0,
        tiled=True,
        axis_index_groups=[[2 * i + e for i in range(half)] for e in range(2)],
    )
    band = rows // count
    return pl.pallas_call(
        compose_kernel,
        out_shape=(
            jax.ShapeDtypeStruct((3, band, cols), f32),
            jax.ShapeDtypeStruct((band, cols), f32),
        ),
        in_specs=[vmem, vmem],
        out_specs=(vmem, vmem),
        name="compose",
    )(consts, pieces)


def solution(mesh):
    placed = (P("gz", "gx", "gy"), P(), P(), P())
    return jax.shard_map(
        on_device,
        mesh=mesh,
        in_specs=placed,
        out_specs=(P(None, ("gx", "gz"), "gy"), P(("gx", "gz"), "gy")),
        check_vma=False,
    )
```
